128 devices in a mesh: dp: 2 (over y_lo), cp: 8 (over y_hi, x), sp: 8 (over z, core).
Axes of the slice: x: 4, y: 4 (y_hi: 2, y_lo: 2; y = y_hi * 2 + y_lo), z: 4, core: 2. Of those that a mesh axis runs over, the one named last changes fastest.
Arguments:
- tokens: bfloat16 [4, 4096, 1024], P('dp', ('cp', 'sp')), may hold values from -6 to 6
- cotangent: bfloat16 [4, 4096, 1024], P('dp', ('cp', 'sp')), may hold values from -6 to 6
- block_of: int32 [16], replicated, may hold values from 0 to 15, as said below
- attn_gain: bfloat16 [1024], P(('dp', 'cp', 'sp')), may hold values from 0.099609375 to 1.8984375
- ffn_gain: bfloat16 [1024], P(('dp', 'cp', 'sp')), may hold values from 0.099609375 to 1.8984375
- head_gains: bfloat16 [2, 64], replicated, may hold values from 0.099609375 to 1.8984375
- w_query: bfloat16 [1024, 1024], P(('dp', 'cp', 'sp')), may hold values from -0.1875 to 0.1875
- w_key: bfloat16 [1024, 512], P(('dp', 'cp', 'sp')), may hold values from -0.1875 to 0.1875
- w_value: bfloat16 [1024, 512], P(('dp', 'cp', 'sp')), may hold values from -0.1875 to 0.1875
- w_out: bfloat16 [1024, 1024], P(('dp', 'cp', 'sp')), may hold values from -3 to 3
- w_gate: bfloat16 [1024, 4608], P(('dp', 'cp', 'sp')), may hold values from -0.1875 to 0.1875
- w_up: bfloat16 [1024, 4608], P(('dp', 'cp', 'sp')), may hold values from -0.1875 to 0.1875
- w_down: bfloat16 [4608, 1024], P(('dp', 'cp', 'sp')), may hold values from -0.09375 to 0.09375
Outputs:
- mixed: bfloat16 [4, 4096, 1024], P('dp', ('cp', 'sp'))
- grad_tokens: bfloat16 [4, 4096, 1024], P('dp', ('cp', 'sp'))
- grad_attn_gain: float32 [1024], P(('dp', 'cp', 'sp'))
- grad_ffn_gain: float32 [1024], P(('dp', 'cp', 'sp'))
- grad_head_gains: float32 [2, 64], replicated
- grad_w_query: float32 [1024, 1024], P(('dp', 'cp', 'sp'))
- grad_w_key: float32 [1024, 512], P(('dp', 'cp', 'sp'))
- grad_w_value: float32 [1024, 512], P(('dp', 'cp', 'sp'))
- grad_w_out: float32 [1024, 1024], P(('dp', 'cp', 'sp'))
- grad_w_gate: float32 [1024, 4608], P(('dp', 'cp', 'sp'))
- grad_w_up: float32 [1024, 4608], P(('dp', 'cp', 'sp'))
- grad_w_down: float32 [4608, 1024], P(('dp', 'cp', 'sp'))
The draws below stay inside these ranges and needn't reach their ends.
Inputs may be any that keep to these rules, and one draw needn't show every extreme that they name: block_of is a permutation of the 16 blocks; slots 2r and 2r + 1 hold two blocks whose numbers add to 15.
All inputs are finite; a program needn't handle non-finite values.
Results may differ from the reference program's by a relative error of at most 0.038.
Values may be sent and summed in bfloat16 or wider, within the bound.
No kernel may reach another device: no remote copies, remote signals or barrier semaphores. Data moves between devices by JAX's collectives and lax.ppermute only.
A program may use at most 448 MiB of HBM per device.

```python
import jax
import jax.numpy as jnp
from jax import lax

D = 1024
HEADS = 16
KVH = 8
HD = 64
FF = 4608
SEQS = 4
SEQ_LEN = 4096
NBLK = 16
BLK = 256


def draw_block_of(key, part):
    key = jax.random.fold_in(key, 11)
    order_key, flip_key = jax.random.split(key)
    pair_count = NBLK // 2
    pairs = jax.random.permutation(order_key, pair_count).astype(jnp.int32)
    flips = jax.random.randint(flip_key, (pair_count,), 0, 2, dtype=jnp.int32)
    first_block = jnp.where(flips == 1, NBLK - 1 - pairs, pairs)
    second_block = NBLK - 1 - first_block
    return jnp.stack([first_block, second_block], axis=1).reshape(NBLK).astype(jnp.int32)


def shard_levels(rng, dims, pieces, smallest, top_value):
    loudness = 1.0
    for position, blocks in pieces:
        heights = jax.random.uniform(jax.random.fold_in(jax.random.fold_in(rng, 6), position), (blocks,), jnp.float32, smallest / len(pieces), top_value / len(pieces))
        loudness = loudness * jnp.repeat(jnp.exp(heights), dims[position] // blocks).reshape((-1,) + (1,) * (len(dims) - 1 - position))
    return loudness


def noise(key, dims, deviation, limit, shards=(), held_as=jnp.bfloat16):
    array = deviation * jax.random.normal(key, dims, jnp.float32)
    if shards:
        array = array * shard_levels(key, dims, shards, -0.22, 0.18)
    return jnp.clip(array, -limit, limit).astype(held_as)


def setup_inputs(seed: int = 0) -> dict:
    streams_of = jax.random.split(jax.random.key(seed), 14)
    tokens = noise(streams_of[0], (SEQS, SEQ_LEN, D), 1.0, 6.0, ((0, 2), (1, 64)))
    cotangent = noise(streams_of[1], (SEQS, SEQ_LEN, D), 1.0, 6.0, ((0, 2), (1, 64)))
    block_of = draw_block_of(jax.random.fold_in(streams_of[13], 71), 0)
    attn_gain = jnp.clip(1.0 + 0.18 * jax.random.normal(streams_of[3], (D,), jnp.float32), 0.099609375, 1.8984375).astype(jnp.bfloat16)
    ffn_gain = jnp.clip(1.0 + 0.18 * jax.random.normal(streams_of[4], (D,), jnp.float32), 0.099609375, 1.8984375).astype(jnp.bfloat16)
    head_gains = jnp.clip(1.0 + 0.18 * jax.random.normal(streams_of[5], (2, HD), jnp.float32), 0.099609375, 1.8984375).astype(jnp.bfloat16)
    w_query = noise(streams_of[6], (D, HEADS * HD), D ** -0.5, 0.1875, ((0, 128),))
    w_key = noise(streams_of[7], (D, KVH * HD), D ** -0.5, 0.1875, ((0, 128),))
    w_value = noise(streams_of[8], (D, KVH * HD), D ** -0.5, 0.1875, ((0, 128),))
    w_out = noise(streams_of[9], (HEADS * HD, D), (max(D * 16 // SEQ_LEN, 1)) ** -0.5, 3.0, ((0, 128),))
    w_gate = noise(streams_of[10], (D, FF), D ** -0.5, 0.1875, ((0, 128),))
    w_up = noise(streams_of[11], (D, FF), D ** -0.5, 0.1875, ((0, 128),))
    w_down = noise(streams_of[12], (FF, D), FF ** -0.5, 0.09375, ((0, 128),))
    return dict(tokens=tokens, cotangent=cotangent, block_of=block_of, attn_gain=attn_gain, ffn_gain=ffn_gain, head_gains=head_gains, w_query=w_query, w_key=w_key, w_value=w_value, w_out=w_out, w_gate=w_gate, w_up=w_up, w_down=w_down)


@jax.custom_vjp
def low(v):
    return lax.optimization_barrier(v.astype(jnp.bfloat16)).astype(jnp.float32)

@jax.custom_vjp
def low_back(v):
    return v

def low_keep(v):
    return (low(v), None)

def low_pass(kept, grad):
    return (grad,)

def back_keep(v):
    return (v, None)

def back_low(kept, grad):
    return (low(grad),)
low.defvjp(low_keep, low_pass)
low_back.defvjp(back_keep, back_low)
EPSILON = 1e-05
NEG_FILL = -1e+30
HIGHEST = lax.Precision.HIGHEST
ROPE_BASE = 1000000.0

def rms_scale(values, gain):
    return values * lax.rsqrt(lax.optimization_barrier(jnp.mean(values * values, axis=-1, keepdims=True)) + EPSILON) * gain

def product_high(left, right):
    return jnp.dot(left, right, precision=HIGHEST, preferred_element_type=jnp.float32)

def rope_tables(positions):
    half = HD // 2
    inverse = ROPE_BASE ** (-(2.0 * jnp.arange(half, dtype=jnp.float32)) / HD)
    angle = positions.astype(jnp.float32)[:, None] * inverse[None, :]
    cosine = jnp.concatenate([jnp.cos(angle), jnp.cos(angle)], axis=-1)[:, None, :]
    sine = jnp.concatenate([jnp.sin(angle), jnp.sin(angle)], axis=-1)[:, None, :]
    return (cosine, sine)

def rotate(values, cosine, sine):
    half = values.shape[-1] // 2
    turned = jnp.concatenate([-values[..., half:], values[..., :half]], axis=-1)
    return values * cosine + turned * sine

def sequence_forward(tokens_seq, params, positions):
    attn_gain, ffn_gain, head_gains, w_query, w_key, w_value, w_out, w_gate, w_up, w_down = params
    group_size = HEADS // KVH
    score_scale = HD ** (-0.5)
    cosine, sine = rope_tables(positions)
    normed = low(rms_scale(tokens_seq, attn_gain))
    query_raw = low_back(product_high(normed, w_query)).reshape(SEQ_LEN, HEADS, HD)
    key_raw = low_back(product_high(normed, w_key)).reshape(SEQ_LEN, KVH, HD)
    query = low_back(low(rotate(rms_scale(query_raw, head_gains[0]), cosine, sine)))
    key_heads = low_back(low(rotate(rms_scale(key_raw, head_gains[1]), cosine, sine)))
    values = low_back(low(product_high(normed, w_value))).reshape(SEQ_LEN, KVH, HD)
    key_repeat = jnp.repeat(key_heads, group_size, axis=1)
    value_repeat = jnp.repeat(values, group_size, axis=1)

    def attend(blocks):
        query_block, query_pos = blocks
        scores = jnp.einsum('qhd,khd->hqk', query_block, key_repeat, precision=HIGHEST)
        scores = low_back(scores * score_scale)
        allowed = positions[None, None, :] <= query_pos[None, :, None]
        scores = jnp.where(allowed, scores, NEG_FILL)
        row_peak = lax.optimization_barrier(jnp.max(scores, axis=-1, keepdims=True))
        weights = jnp.exp(scores - row_peak)
        probabilities = low(weights / lax.optimization_barrier(jnp.sum(weights, axis=-1, keepdims=True)))
        return jnp.einsum('hqk,khd->qhd', probabilities, value_repeat, precision=HIGHEST)
    attended = lax.map(jax.checkpoint(attend), (query.reshape(NBLK, BLK, HEADS, HD), positions.reshape(NBLK, BLK)))
    attended = low_back(low(attended.reshape(SEQ_LEN, HEADS * HD)))
    branch = low_back(product_high(attended, w_out))
    middle = tokens_seq + branch
    normed_ffn = low(rms_scale(middle, ffn_gain))
    gate_pre = low_back(product_high(normed_ffn, w_gate))
    up_pre = low_back(product_high(normed_ffn, w_up))
    hidden = low(jax.nn.silu(gate_pre) * up_pre)
    return middle + product_high(hidden, w_down)

def reference(tokens, cotangent, block_of, attn_gain, ffn_gain, head_gains, w_query, w_key, w_value, w_out, w_gate, w_up, w_down):
    row_index = jnp.arange(SEQ_LEN, dtype=jnp.int32)
    positions = (block_of[row_index // BLK] * BLK + row_index % BLK).astype(jnp.int32)
    params = tuple((array_in.astype(jnp.float32) for array_in in (attn_gain, ffn_gain, head_gains, w_query, w_key, w_value, w_out, w_gate, w_up, w_down)))

    def forward(inputs, *weights_in):
        return lax.map(lambda sequence: sequence_forward(sequence, weights_in, positions), inputs)
    output, pullback = jax.vjp(forward, tokens.astype(jnp.float32), *params)
    gradients = pullback(cotangent.astype(jnp.float32))
    return (output.astype(jnp.bfloat16), gradients[0].astype(jnp.bfloat16), gradients[1], gradients[2], gradients[3], gradients[4], gradients[5], gradients[6], gradients[7], gradients[8], gradients[9], gradients[10])
```

```python
from functools import partial

import jax
import jax.numpy as jnp
from jax import lax
from jax.experimental import pallas as pl
from jax.experimental.pallas import tpu as pltpu
from jax.sharding import Mesh
from jax.sharding import PartitionSpec as P

SP = ("sp_0", "sp_1")
DC = ("dp", "cp_0", "cp_1")
SEQ_Z = ("cp_0", "sp_0")
DP_CP_SP = ("dp", "cp_0", "cp_1", "sp_0", "sp_1")
CP_SP = ("cp_0", "cp_1", "sp_0", "sp_1")

EPSILON = 1e-05
ROPE_BASE = 1000000.0
BF = jnp.bfloat16
F32 = jnp.float32

D = 1024
HD = 64
FF = 4608
FS = FF // 8
FP = 640
BLK = 256
ROWS = 1024
TILE = 256
VMEM_LIMIT = 56 * 1024 * 1024


def dot(left, right):
    return jnp.dot(left, right, preferred_element_type=F32)


def dot_rows(left, right):
    return lax.dot_general(left, right, (((0,), (0,)), ((), ())), preferred_element_type=F32)


def dot_cols(left, right):
    return lax.dot_general(left, right, (((1,), (1,)), ((), ())), preferred_element_type=F32)


def call(body, out, **kw):
    flops = kw.pop("flops", 0)
    nbytes = kw.pop("nbytes", 0)
    return pl.pallas_call(
        body,
        out_shape=out,
        compiler_params=pltpu.CompilerParams(vmem_limit_bytes=VMEM_LIMIT),
        cost_estimate=pl.CostEstimate(flops=flops, bytes_accessed=nbytes, transcendentals=0),
        **kw,
    )


def shaped(shape, dtype):
    return jax.ShapeDtypeStruct(shape, dtype)


def sibling(x):
    return lax.ppermute(x, "sp_1", [(0, 1), (1, 0)])


def exchange(x, axis):
    return lax.all_to_all(x, axis, 0, 0, tiled=True)


def spread_rows(rows):
    mine = exchange(jnp.repeat(rows, 4, axis=0), SEQ_Z)
    return jnp.stack([mine, sibling(mine)])


def collect_rows(part):
    half = part[0].astype(F32) + sibling(part[1]).astype(F32)
    terms = exchange(half.astype(BF), SEQ_Z)
    return jnp.sum(terms.reshape(2, 4, 64, -1).astype(F32), axis=1)


def rms_of(x):
    return lax.rsqrt(jnp.mean(x * x, axis=-1, keepdims=True) + EPSILON)


def norm_back(x, gain, upstream):
    r = rms_of(x)
    n = x * r
    scaled = upstream * gain
    grad = r * (scaled - n * jnp.mean(scaled * n, axis=-1, keepdims=True))
    return grad, jnp.sum(upstream * n, axis=0, keepdims=True)


def low_half(shape):
    return lax.broadcasted_iota(jnp.int32, shape, 1) < HD


def head_mean(v):
    low = low_half(v.shape)
    first = jnp.sum(jnp.where(low, v, 0.0), axis=1, keepdims=True)
    second = jnp.sum(jnp.where(low, 0.0, v), axis=1, keepdims=True)
    return jnp.where(low, first, second) * (1.0 / HD)


def swap_halves(v):
    lane = lax.broadcasted_iota(jnp.int32, v.shape, 1)
    return jnp.where(lane % HD < HD // 2, pltpu.roll(v, 96, 1), pltpu.roll(v, 32, 1))


def row_tables(block_of, core):
    cycle = lax.axis_index("cp_1")
    pairs = lax.dynamic_index_in_dim(block_of.reshape(2, 4, 2), cycle, 1, keepdims=False)
    half = HD // 2
    inverse = ROPE_BASE ** (-(2.0 * jnp.arange(half, dtype=F32)) / HD)
    inverse = jnp.tile(inverse, 4)
    sign = jnp.tile(jnp.concatenate([-jnp.ones(half, F32), jnp.ones(half, F32)]), 2)
    first = (pairs.reshape(4) * BLK).astype(F32)[:, None] * inverse[None]
    rel = jnp.arange(2, dtype=jnp.int32)[:, None, None]
    zz = jnp.arange(2, dtype=jnp.int32)[None, :, None]
    row = jnp.arange(64, dtype=jnp.int32)[None, None, :]
    inner = (zz * 128 + (rel ^ core) * 64 + row).reshape(256).astype(F32)[:, None] * inverse[None]
    ca, sa = jnp.cos(first).reshape(1, 2, 2, 1, 1, 128), jnp.sin(first).reshape(1, 2, 2, 1, 1, 128)
    cb, sb = jnp.cos(inner).reshape(2, 1, 1, 2, 64, 128), jnp.sin(inner).reshape(2, 1, 1, 2, 64, 128)
    cosine = (ca * cb - sa * sb).reshape(ROWS, 128)
    sine = ((sa * cb + ca * sb) * sign).reshape(ROWS, 128)
    return cosine, sine, pairs


def project_body(x_ref, gain_ref, w_ref, cos_ref, sin_ref, gq_ref, gk_ref, n_ref, raw_ref, q_ref, kv_ref):
    x = x_ref[...].astype(F32)
    normed = (x * rms_of(x) * gain_ref[...].astype(F32)).astype(BF)
    n_ref[...] = normed
    raw = dot(normed, w_ref[...])
    raw_ref[...] = raw
    cosine, sine = cos_ref[...], sin_ref[...]

    def turned(v, gain):
        v = v * lax.rsqrt(head_mean(v * v) + EPSILON) * gain
        return (v * cosine + swap_halves(v) * sine).astype(BF)

    q_ref[...] = turned(raw[:, :128], gq_ref[...]) * jnp.asarray(0.125, BF)
    right = raw[:, 128:]
    kv_ref[...] = jnp.where(low_half(right.shape), turned(right, gk_ref[...]), right.astype(BF))


def tiles(width):
    return pl.BlockSpec((TILE, width), lambda t: (t, 0))


def whole(*shape):
    return pl.BlockSpec(shape, lambda t: (0,) * len(shape))


def project(x, gain, w, cosine, sine, gq, gk):
    return call(
        project_body,
        (
            shaped((ROWS, D), BF),
            shaped((ROWS, 256), F32),
            shaped((ROWS, 128), BF),
            shaped((ROWS, 128), BF),
        ),
        grid=(ROWS // TILE,),
        in_specs=[tiles(D), whole(1, D), whole(D, 256), tiles(128), tiles(128), whole(1, 128), whole(1, 128)],
        out_specs=(tiles(D), tiles(256), tiles(128), tiles(128)),
        flops=2 * ROWS * D * 256,
        nbytes=7 * 2**20,
        name="project",
    )(x, gain, w, cosine, sine, gq, gk)


def project_back_body(
    dq_ref, dkv_ref, raw_ref, cos_ref, sin_ref, gq_ref, gk_ref, n_ref, x_ref, gain_ref, w_ref,
    part_ref, gw_ref, ggain_ref, ghead_ref, gw_acc,
):
    step = pl.program_id(0)

    @pl.when(step == 0)
    def _():
        gw_acc[...] = jnp.zeros_like(gw_acc)
        ggain_ref[...] = jnp.zeros_like(ggain_ref)
        ghead_ref[...] = jnp.zeros_like(ghead_ref)

    cosine, sine = cos_ref[...], sin_ref[...]

    def back(raw, grad, gain):
        r = lax.rsqrt(head_mean(raw * raw) + EPSILON)
        n = raw * r
        up = grad * cosine + swap_halves(grad * sine)
        scaled = up * gain
        return r * (scaled - n * head_mean(scaled * n)), jnp.sum(up * n, axis=0, keepdims=True)

    raw = raw_ref[...]
    graw_q, gain_q = back(raw[:, :128], dq_ref[...], gq_ref[...])
    dkv = dkv_ref[...]
    graw_k, gain_k = back(raw[:, 128:], dkv, gk_ref[...])
    ghead_ref[...] += jnp.concatenate([gain_q, gain_k], axis=0)
    graw = jnp.concatenate([graw_q, jnp.where(low_half(dkv.shape), graw_k, dkv)], axis=1).astype(BF)
    gw_acc[...] += dot_rows(n_ref[...], graw)
    part, ggain = norm_back(
        x_ref[...].astype(F32), gain_ref[...].astype(F32), dot_cols(graw, w_ref[...])
    )
    part_ref[...] = part.astype(BF)
    ggain_ref[...] += ggain

    @pl.when(step == pl.num_programs(0) - 1)
    def _():
        gw_ref[...] = gw_acc[...].astype(BF)


def project_back(dq, dkv, raw, cosine, sine, gq, gk, normed, x, gain, w):
    return call(
        project_back_body,
        (
            shaped((ROWS, D), BF),
            shaped((D, 256), BF),
            shaped((1, D), F32),
            shaped((2, 128), F32),
        ),
        grid=(ROWS // TILE,),
        in_specs=[
            tiles(128), tiles(128), tiles(256), tiles(128), tiles(128), whole(1, 128), whole(1, 128),
            tiles(D), tiles(D), whole(1, D), whole(D, 256),
        ],
        out_specs=(tiles(D), whole(D, 256), whole(1, D), whole(2, 128)),
        scratch_shapes=[pltpu.VMEM((D, 256), F32)],
        flops=4 * ROWS * D * 256,
        nbytes=11 * 2**20,
        name="project_back",
    )(dq, dkv, raw, cosine, sine, gq, gk, normed, x, gain, w)


def stored(ref, block, o, h):
    rows = ref[block, :, pl.ds(o * 4 + h * 2, 2)] if block is not None else ref[:, pl.ds(o * 4 + h * 2, 2)]
    return rows.reshape(BLK, 128)


def heads_across(block):
    flat = block.astype(F32).T
    return jnp.concatenate([flat[:HD], flat[HD:]], axis=1)


def diagonal_mask(core):
    def place(t):
        return ((t >> 6) & 1) * 128 + ((t >> 7) ^ core) * 64 + (t & 63)

    keys = place(lax.broadcasted_iota(jnp.int32, (BLK, 2 * BLK), 0))
    queries = place(lax.broadcasted_iota(jnp.int32, (BLK, 2 * BLK), 1) & 255)
    return keys <= queries


def pair_at(tab_ref, i, o):
    count = tab_ref[2 * o]
    first = i < count
    qb = 2 * o + jnp.where(first, 0, 1)
    slot = tab_ref[8 + jnp.where(first, i, i - count)]
    return qb, slot


def attend_body(tab_ref, q_ref, kv_ref, att_ref, attT_ref, lse_ref, qT, kv, vT, acc):
    zeros = jnp.zeros((HD, 2 * BLK), BF)
    for qb in range(4):
        qT[qb, :HD] = heads_across(stored(q_ref, None, qb // 2, qb % 2)).astype(BF)
        qT[qb, HD:] = zeros
    for slot in range(16):
        block = stored(kv_ref, (slot >> 1) & 3, slot >> 3, slot & 1)
        kv[slot] = block
        flat = block.astype(F32).T
        vT[slot] = jnp.concatenate([jnp.ones((16, BLK), F32), flat[HD:]], axis=0).astype(BF)
    acc[...] = jnp.zeros_like(acc)

    def pair(qb, slot, mask=None):
        p = jnp.exp(dot(kv[slot], qT[qb]))
        if mask is not None:
            p = jnp.where(mask, p, 0.0)
        acc[qb] += dot(vT[slot], p.astype(BF))

    def step(i, carry):
        for o in range(2):
            pair(*pair_at(tab_ref, i, o))
        return carry

    lax.fori_loop(0, 15, step, 0)
    mask = diagonal_mask(tab_ref[4])
    for qb in range(4):
        pair(qb, tab_ref[8 + tab_ref[qb]], mask)
        total = acc[qb, :1]
        out = acc[qb, 16:] / total
        flat = jnp.concatenate([out[:, :BLK], out[:, BLK:]], axis=0)
        attT_ref[qb] = flat
        lse_ref[qb] = jnp.log(total)
        att_ref[:, pl.ds((qb // 2) * 4 + (qb % 2) * 2, 2)] = flat.T.astype(BF).reshape(2, 2, 64, 128)


def in_smem():
    return pl.BlockSpec(memory_space=pltpu.SMEM)


def in_vmem():
    return pl.BlockSpec(memory_space=pltpu.VMEM)


def attend(table, q, kv):
    return call(
        attend_body,
        (
            shaped((2, 8, 64, 128), BF),
            shaped((4, 128, BLK), F32),
            shaped((4, 1, 2 * BLK), F32),
        ),
        in_specs=[in_smem(), in_vmem(), in_vmem()],
        out_specs=(in_vmem(), in_vmem(), in_vmem()),
        scratch_shapes=[
            pltpu.VMEM((4, 128, 2 * BLK), BF),
            pltpu.VMEM((16, BLK, 128), BF),
            pltpu.VMEM((16, HD + 16, BLK), BF),
            pltpu.VMEM((4, HD + 16, 2 * BLK), F32),
        ],
        flops=34 * 4 * BLK * 2 * BLK * 128,
        nbytes=2 * 2**20,
        name="attend",
    )(table, q, kv)


def attend_back_body(
    tab_ref, q_ref, kv_ref, g_ref, attT_ref, lse_ref, dq_ref, dkv_ref,
    qT, gT, qn, gn, kv, kT, delta, dqT, dkv,
):
    zeros = jnp.zeros((HD, 2 * BLK), F32)
    for qb in range(4):
        across = jnp.concatenate([heads_across(stored(q_ref, None, qb // 2, qb % 2)), zeros], axis=0)
        qT[qb] = across.astype(BF)
        qn[qb] = across.T.astype(BF)
        g_across = heads_across(stored(g_ref, None, qb // 2, qb % 2))
        out = attT_ref[qb]
        out = jnp.concatenate([out[:HD], out[HD:]], axis=1)
        delta[qb] = jnp.sum(g_across * out, axis=0, keepdims=True)
        g_across = jnp.concatenate([zeros, g_across], axis=0)
        gT[qb] = g_across.astype(BF)
        gn[qb] = g_across.T.astype(BF)
    for slot in range(16):
        block = stored(kv_ref, (slot >> 1) & 3, slot >> 3, slot & 1)
        kv[slot] = block
        kT[slot] = block.astype(F32).T[:HD].astype(BF)
    dqT[...] = jnp.zeros_like(dqT)
    dkv[...] = jnp.zeros_like(dkv)

    def pair(qb, slot, mask=None):
        keys = kv[slot]
        p = jnp.exp(dot(keys, qT[qb]) - lse_ref[qb])
        if mask is not None:
            p = jnp.where(mask, p, 0.0)
        ds = (p * (dot(keys, gT[qb]) - delta[qb])).astype(BF)
        dkv[slot] += dot(ds, qn[qb]) + dot(p.astype(BF), gn[qb])
        dqT[qb] += dot(kT[slot], ds)

    def step(i, carry):
        for o in range(2):
            pair(*pair_at(tab_ref, i, o))
        return carry

    lax.fori_loop(0, 15, step, 0)
    mask = diagonal_mask(tab_ref[4])
    for qb in range(4):
        pair(qb, tab_ref[8 + tab_ref[qb]], mask)
        flat = jnp.concatenate([dqT[qb, :, :BLK], dqT[qb, :, BLK:]], axis=0)
        dq_ref[:, pl.ds((qb // 2) * 4 + (qb % 2) * 2, 2)] = (flat.T * 0.125).reshape(2, 2, 64, 128)
    for slot in range(16):
        dkv_ref[(slot >> 1) & 3, :, pl.ds((slot >> 3) * 4 + (slot & 1) * 2, 2)] = (
            dkv[slot].astype(BF).reshape(2, 2, 64, 128)
        )


def attend_back(table, q, kv, g, attT, lse):
    return call(
        attend_back_body,
        (shaped((2, 8, 64, 128), F32), shaped((4, 2, 8, 64, 128), BF)),
        in_specs=[in_smem()] + [in_vmem()] * 5,
        out_specs=(in_vmem(), in_vmem()),
        scratch_shapes=[
            pltpu.VMEM((4, 128, 2 * BLK), BF),
            pltpu.VMEM((4, 128, 2 * BLK), BF),
            pltpu.VMEM((4, 2 * BLK, 128), BF),
            pltpu.VMEM((4, 2 * BLK, 128), BF),
            pltpu.VMEM((16, BLK, 128), BF),
            pltpu.VMEM((16, HD, BLK), BF),
            pltpu.VMEM((4, 1, 2 * BLK), F32),
            pltpu.VMEM((4, HD, 2 * BLK), F32),
            pltpu.VMEM((16, BLK, 128), F32),
        ],
        flops=34 * 10 * BLK * 2 * BLK * 128,
        nbytes=4 * 2**20,
        name="attend_back",
    )(table, q, kv, g, attT, lse)


def ffn_body(
    place_ref, x_ref, own_ref, other_ref, g_ref, gain_ref, wo_ref, wgu_ref, wd_ref,
    mixed_ref, part_ref, gwgu_ref, gwd_ref, ggain_ref, gwgu, gwd,
):
    step = pl.program_id(0)

    @pl.when(step == 0)
    def _():
        gwgu[...] = jnp.zeros_like(gwgu)
        gwd[...] = jnp.zeros_like(gwd)
        ggain_ref[...] = jnp.zeros_like(ggain_ref)

    core = place_ref[0]
    pieces = []
    for z in range(4):
        own, other = own_ref[z], other_ref[z]
        pieces += [jnp.where(core == 0, own, other), jnp.where(core == 0, other, own)]
    middle = x_ref[...].astype(F32) + dot(jnp.concatenate(pieces, axis=1), wo_ref[...])
    gain = gain_ref[...].astype(F32)
    normed = (middle * rms_of(middle) * gain).astype(BF)
    pre = dot(normed, wgu_ref[...])
    gate, up = pre[:, :FP], pre[:, FP:]
    s = 1.0 / (1.0 + jnp.exp(-gate))
    act = gate * s
    hidden = (act * up).astype(BF)
    row = lax.broadcasted_iota(jnp.int32, (TILE, 1), 0) >> 6
    here = jnp.logical_and(step < 2, row == place_ref[1])
    mixed_ref[...] = (dot(hidden, wd_ref[...]) + jnp.where(here, middle, 0.0)).astype(BF)
    g = g_ref[...]
    gh = dot_cols(g, wd_ref[...])
    gwd[...] += dot_rows(hidden, g)
    gpre = jnp.concatenate([gh * up * s * (1.0 + gate * (1.0 - s)), gh * act], axis=1).astype(BF)
    gwgu[...] += dot_rows(normed, gpre)
    part, ggain = norm_back(middle, gain, dot_cols(gpre, wgu_ref[...]))
    part_ref[...] = part.astype(BF)
    ggain_ref[...] += ggain

    @pl.when(step == pl.num_programs(0) - 1)
    def _():
        gwgu_ref[...] = gwgu[...].astype(BF)
        gwd_ref[...] = gwd[...].astype(BF)


def ffn(place, x, own, other, g, gain, wo, wgu, wd):
    def of_other(t):
        return (0, (t + 2) % 4, 0)

    return call(
        ffn_body,
        (
            shaped((ROWS, D), BF),
            shaped((ROWS, D), BF),
            shaped((D, 2 * FP), BF),
            shaped((FP, D), BF),
            shaped((1, D), F32),
        ),
        grid=(ROWS // TILE,),
        in_specs=[
            in_smem(),
            tiles(D),
            pl.BlockSpec((4, TILE, 128), lambda t: (0, t, 0)),
            pl.BlockSpec((4, TILE, 128), of_other),
            tiles(D),
            whole(1, D),
            whole(D, D),
            whole(D, 2 * FP),
            whole(FP, D),
        ],
        out_specs=(tiles(D), tiles(D), whole(D, 2 * FP), whole(FP, D), whole(1, D)),
        scratch_shapes=[pltpu.VMEM((D, 2 * FP), F32), pltpu.VMEM((FP, D), F32)],
        flops=2 * ROWS * D * (D + 9 * FP),
        nbytes=24 * 2**20,
        name="ffn",
    )(place, x, own, other, g, gain, wo, wgu, wd)


def column_slices(w):
    return jnp.transpose(w.reshape(8, 8, -1), (1, 0, 2))


def gather_all(x):
    r, width = x.shape
    over = exchange(jnp.broadcast_to(x[None], (16, r, width)), DC)
    own = exchange(jnp.broadcast_to(over[None], (4, 16, r, width)).reshape(64, r, width), "sp_0")
    own = own.reshape(4, 16, r, width)
    other = sibling(own)
    core = lax.axis_index("sp_1")
    both = jnp.stack([jnp.where(core == 0, own, other), jnp.where(core == 0, other, own)], axis=1)
    return jnp.transpose(both, (2, 0, 1, 3, 4)).reshape(128 * r, width)


def on_device(
    tokens, cotangent, block_of, attn_gain, ffn_gain, head_gains,
    w_query, w_key, w_value, w_out, w_gate, w_up, w_down,
):
    core = lax.axis_index("sp_1")
    z = lax.axis_index("sp_0")
    s_index = lax.axis_index(SP)
    gains_f = head_gains.astype(F32)
    gq = jnp.tile(gains_f[0], 2)[None]
    gk = jnp.tile(gains_f[1], 2)[None]
    cosine, sine, pairs = row_tables(block_of, core)
    slots = jnp.arange(16, dtype=jnp.int32)
    slot_at = jnp.sum(jnp.where(block_of[None, :] == slots[:, None], slots[None, :], 0), axis=1)
    table = jnp.concatenate(
        [pairs.reshape(4), jnp.stack([core, core, core, core]), slot_at]
    ).astype(jnp.int32)

    qkv = jnp.concatenate([column_slices(w) for w in (w_query, w_key, w_value)], axis=2)
    gains = jnp.pad(jnp.concatenate([attn_gain, ffn_gain])[None, None], ((0, 0), (0, 7), (0, 240)))
    qkv = jnp.concatenate([qkv, jnp.broadcast_to(gains, (8, 8, 256))], axis=1)
    qkv = exchange(qkv, SP)
    gains = jnp.pad(qkv[:, 8, :16].reshape(1, 128), ((0, 7), (0, 128)))
    qkv = jnp.concatenate([qkv[:, :8].reshape(64, 256), gains], axis=0)
    qkv = exchange(jnp.broadcast_to(qkv[None], (16, 72, 256)), DC)
    w_qkv = qkv[:, :64].reshape(D, 256)
    gains = qkv[:, 64, :128].reshape(16, 8, 16)
    gain_attn = gains[:, :, :8].reshape(1, D)
    gain_ffn = gains[:, :, 8:].reshape(1, D)

    x_all = spread_rows(tokens).reshape(ROWS, D)
    normed, raw, q, kv = project(x_all, gain_attn, w_qkv, cosine, sine, gq, gk)
    kv_all = exchange(jnp.broadcast_to(kv.reshape(1, ROWS, 128), (4, ROWS, 128)), "cp_1")
    kv_all = kv_all.reshape(4, 2, 8, 64, 128)
    q = q.reshape(2, 8, 64, 128)

    pad = ((0, 0), (0, 0), (0, FP - FS))
    gu = jnp.concatenate([jnp.pad(column_slices(w), pad) for w in (w_gate, w_up)], axis=2)
    gu = exchange(gu, SP).reshape(64, 2 * FP)
    w_gu = lax.all_gather(gu, DC, axis=0, tiled=True)
    perm = [(d, (d % 16) * 8 + d // 16) for d in range(128)]
    down = lax.ppermute(w_down, DP_CP_SP, perm)
    down = lax.all_gather(down, DC, axis=0, tiled=True)
    w_dn = jnp.pad(down, ((0, FP - FS), (0, 0)))
    w_o = gather_all(w_out)

    att, attT, lse = attend(table, q, kv_all)
    own = exchange(jnp.broadcast_to(att.reshape(1, ROWS, 128), (4, ROWS, 128)), "sp_0")
    other = sibling(own)
    g_all = spread_rows(cotangent).reshape(ROWS, D)
    place = jnp.stack([core, z]).astype(jnp.int32)
    mixed_part, mid_part, gw_gu, gw_dn, gg_ffn = ffn(
        place, x_all, own, other, g_all, gain_ffn, w_o, w_gu, w_dn
    )
    grad_middle = cotangent.astype(F32) + collect_rows(mid_part.reshape(2, 8, 64, D))
    gb_all = spread_rows(grad_middle.astype(BF)).reshape(ROWS, D)
    w_o_mine = lax.dynamic_slice_in_dim(w_o, s_index * 128, 128, 0)
    grad_att = dot_cols(gb_all, w_o_mine).astype(BF)
    dq, dkv = attend_back(table, q, kv_all, grad_att.reshape(2, 8, 64, 128), attT, lse)
    dkv = exchange(dkv.reshape(4, ROWS, 128), "cp_1")
    dkv = jnp.sum(dkv.astype(F32), axis=0)
    part, gw_qkv, gg_attn, gg_head = project_back(
        dq.reshape(ROWS, 128), dkv, raw, cosine, sine, gq, gk, normed, x_all, gain_attn, w_qkv
    )
    grad_tokens = (grad_middle + collect_rows(part.reshape(2, 8, 64, D))).astype(BF)
    mixed = collect_rows(mixed_part.reshape(2, 8, 64, D)).astype(BF)

    gw_out = dot_rows(att.reshape(ROWS, 128), gb_all).astype(BF)
    back = [(d, s) for s, d in perm]
    downs = jnp.concatenate([gw_dn[:FS].reshape(16, 36, D), gw_out.reshape(16, 8, D)], axis=1)
    downs = jnp.pad(downs, ((0, 0), (0, 4), (0, 0)))
    downs = lax.psum_scatter(downs.reshape(16 * 48, D), DC, scatter_dimension=0, tiled=True)
    downs = lax.ppermute(downs, DP_CP_SP, back)
    grad_w_down, grad_w_out = downs[:36].astype(F32), downs[36:44].astype(F32)
    gus = lax.psum_scatter(gw_gu, DC, scatter_dimension=0, tiled=True)
    gus = exchange(gus.reshape(8, 8, 2 * FP), SP)

    def columns(x):
        return jnp.transpose(x, (1, 0, 2)).reshape(8, -1).astype(F32)

    grad_w_gate = columns(gus[:, :, :FS])
    grad_w_up = columns(gus[:, :, FP : FP + FS])

    smalls = jnp.concatenate(
        [
            gg_attn.reshape(16, 64),
            gg_ffn.reshape(16, 64),
            jnp.broadcast_to((gg_head[:, :HD] + gg_head[:, HD:] * jnp.array([[1.0], [0.0]])).reshape(1, 128), (16, 128)),
        ],
        axis=1,
    )
    small_rows = jnp.pad(smalls.astype(BF)[:, None], ((0, 0), (0, 7), (0, 0)))
    lines = jnp.concatenate([gw_qkv.reshape(16, 64, 256), small_rows], axis=1)
    lines = jnp.sum(exchange(lines, DC).astype(F32), axis=0)
    tail = lines[64]
    tail = jnp.concatenate(
        [
            tail[:64].reshape(8, 8),
            tail[64:128].reshape(8, 8),
            jnp.zeros((8, 112), F32),
            jnp.broadcast_to(tail[None, 128:], (8, 128)),
        ],
        axis=1,
    )
    lines = jnp.concatenate([lines[:64].reshape(8, 8, 256), jnp.pad(tail[:, None], ((0, 0), (0, 7), (0, 0)))], axis=1)
    lines = exchange(lines, SP)
    grad_w_query = columns(lines[:, :8, :128])
    grad_w_key = columns(lines[:, :8, 128:192])
    grad_w_value = columns(lines[:, :8, 192:])
    tail = jnp.sum(lines[:, 8], axis=0)
    return (
        mixed,
        grad_tokens,
        tail[:8],
        tail[8:16],
        tail[128:].reshape(2, HD),
        grad_w_query,
        grad_w_key,
        grad_w_value,
        grad_w_out,
        grad_w_gate,
        grad_w_up,
        grad_w_down,
    )


def solution(mesh):
    torus = Mesh(
        mesh.devices.reshape(mesh.shape["dp"], 2, 4, 4, 2), ("dp", "cp_0", "cp_1", "sp_0", "sp_1")
    )
    rows, split = P("dp", CP_SP, None), P(DP_CP_SP, None)
    in_specs = (rows, rows, P(), P(DP_CP_SP), P(DP_CP_SP), P()) + (split,) * 7
    out_specs = (rows, rows, P(DP_CP_SP), P(DP_CP_SP), P()) + (split,) * 7
    return jax.shard_map(
        on_device, mesh=torus, in_specs=in_specs, out_specs=out_specs, check_vma=False
    )
```

```python
from functools import partial

import jax
import jax.numpy as jnp
from jax import lax
from jax.experimental import pallas as pl
from jax.experimental.pallas import tpu as pltpu
from jax.sharding import Mesh
from jax.sharding import PartitionSpec as P

SP = ("sp_0", "sp_1")
DC = ("dp", "cp_0", "cp_1")
DP_CP_SP = ("dp", "cp_0", "cp_1", "sp_0", "sp_1")
CP_SP = ("cp_0", "cp_1", "sp_0", "sp_1")

EPSILON = 1e-05
ROPE_BASE = 1000000.0
BF = jnp.bfloat16
F32 = jnp.float32

D = 1024
HD = 64
FF = 4608
FS = FF // 8
FP = 640
BLK = 256
ROWS = 1024
TILE = 256
VMEM_LIMIT = 56 * 1024 * 1024


def dot(left, right):
    return jnp.dot(left, right, preferred_element_type=F32)


def dot_rows(left, right):
    return lax.dot_general(left, right, (((0,), (0,)), ((), ())), preferred_element_type=F32)


def dot_cols(left, right):
    return lax.dot_general(left, right, (((1,), (1,)), ((), ())), preferred_element_type=F32)


def call(body, out, **kw):
    flops = kw.pop("flops", 0)
    nbytes = kw.pop("nbytes", 0)
    after = kw.pop("after", ())
    if after:
        inner, count = body, len(after)
        kw["in_specs"] = [pl.BlockSpec(memory_space=pl.ANY)] * count + list(kw["in_specs"])

        def body(*refs):
            return inner(*refs[count:])

        return partial(call(body, out, flops=flops, nbytes=nbytes, **kw), *after)
    return pl.pallas_call(
        body,
        out_shape=out,
        compiler_params=pltpu.CompilerParams(vmem_limit_bytes=VMEM_LIMIT),
        cost_estimate=pl.CostEstimate(flops=flops, bytes_accessed=nbytes, transcendentals=0),
        **kw,
    )


def shaped(shape, dtype):
    return jax.ShapeDtypeStruct(shape, dtype)


def ring(x, axis, k):
    return lax.ppermute(x, axis, [(i, (i + k) % 4) for i in range(4)])


def pair(x, axis):
    return lax.ppermute(x, axis, [(0, 1), (1, 0)])


def sibling(x):
    return pair(x, "sp_1")


def exchange(x, axis):
    return lax.all_to_all(x, axis, 0, 0, tiled=True)


def after(x, *first):
    return lax.optimization_barrier((x, *first))[0]


def around(x, axis):
    return [x] + [ring(x, axis, k) for k in (1, 2, 3)]


def own_first(both, half):
    return jnp.where(half == 0, both, both[::-1])


def swapped(rows):
    return jnp.concatenate([rows[0], pair(rows[1], "cp_0")], axis=0)


def sum_cores(own, other):
    came = sibling(other)
    return [
        own[r : r + 128].astype(F32) + came[r : r + 128].astype(F32) for r in range(0, 512, 128)
    ]


def rms_of(x):
    return lax.rsqrt(jnp.mean(x * x, axis=-1, keepdims=True) + EPSILON)


def norm_back(x, gain, upstream):
    r = rms_of(x)
    n = x * r
    scaled = upstream * gain
    return r * (scaled - n * jnp.mean(scaled * n, axis=-1, keepdims=True))


def low_half(shape):
    return lax.broadcasted_iota(jnp.int32, shape, 1) < HD


def head_mean(v):
    low = low_half(v.shape)
    first = jnp.sum(jnp.where(low, v, 0.0), axis=1, keepdims=True)
    second = jnp.sum(jnp.where(low, 0.0, v), axis=1, keepdims=True)
    return jnp.where(low, first, second) * (1.0 / HD)


def swap_halves(v):
    lane = lax.broadcasted_iota(jnp.int32, v.shape, 1)
    return jnp.where(lane % HD < HD // 2, pltpu.roll(v, 96, 1), pltpu.roll(v, 32, 1))


def row_tables(block_of, core, half, cycle, level):
    slots = jnp.arange(16, dtype=jnp.int32)
    blocks = block_of.reshape(2, 4, 2)
    blocks = jnp.where(half == 0, blocks, blocks[::-1])
    local = lax.dynamic_index_in_dim(blocks, cycle, 1, keepdims=False)
    z = (level - jnp.arange(4, dtype=jnp.int32)) % 4
    pick = (z // 2)[None, :] == 1
    by_z = jnp.where(pick, local[:, 1:], local[:, :1]).T
    entries = HD // 2
    inverse = ROPE_BASE ** (-(2.0 * jnp.arange(entries, dtype=F32)) / HD)
    inverse = jnp.tile(inverse, 4)
    sign = jnp.tile(jnp.concatenate([-jnp.ones(entries, F32), jnp.ones(entries, F32)]), 2)
    first = (by_z.reshape(8) * BLK).astype(F32)[:, None] * inverse[None]
    rel = jnp.arange(2, dtype=jnp.int32)[:, None, None]
    row = jnp.arange(64, dtype=jnp.int32)[None, None, :]
    inner = ((z % 2)[None, :, None] * 128 + (rel ^ core) * 64 + row).reshape(512)
    inner = inner.astype(F32)[:, None] * inverse[None]
    ca, sa = (f(first).reshape(1, 4, 2, 1, 128) for f in (jnp.cos, jnp.sin))
    cb, sb = (f(inner).reshape(2, 4, 1, 64, 128) for f in (jnp.cos, jnp.sin))
    cosine = (ca * cb - sa * sb).reshape(ROWS, 128)
    sine = ((sa * cb + ca * sb) * sign).reshape(ROWS, 128)
    distance = (cycle - (slots >> 1)) & 3
    at = distance * 4 + ((slots >> 3) ^ half) * 2 + (slots & 1)
    slot_at = jnp.sum(jnp.where(block_of[None, :] == slots[:, None], at[None, :], 0), axis=1)
    place = (level - jnp.arange(4, dtype=jnp.int32)) & 3
    table = jnp.concatenate([local.reshape(4), place, slot_at, core[None]]).astype(jnp.int32)
    return cosine, sine, table


def project_body(own_ref, other_ref, gain_ref, w_ref, cos_ref, sin_ref, gq_ref, gk_ref, n_ref, raw_ref, q_ref, kv_ref):
    x = picked(own_ref, other_ref).astype(F32)
    normed = (x * rms_of(x) * gain_ref[...].astype(F32)).astype(BF)
    n_ref[...] = normed
    raw = dot(normed, w_ref[:, :64].reshape(D, 256))
    raw_ref[...] = raw
    cosine, sine = cos_ref[...], sin_ref[...]

    def turned(v, gain):
        v = v * lax.rsqrt(head_mean(v * v) + EPSILON) * gain
        return (v * cosine + swap_halves(v) * sine).astype(BF)

    q_ref[...] = turned(raw[:, :128], gq_ref[...]) * jnp.asarray(0.125, BF)
    right = raw[:, 128:]
    kv_ref[...] = jnp.where(low_half(right.shape), turned(right, gk_ref[...]), right.astype(BF))


def picked(own_ref, other_ref):
    return jnp.where(pl.program_id(0) < 2, own_ref[...], other_ref[...])


def halves(width):
    return [
        pl.BlockSpec((TILE, width), lambda t: (jnp.minimum(t, 1), 0)),
        pl.BlockSpec((TILE, width), lambda t: (jnp.maximum(t - 2, 0), 0)),
    ]


def tiles(width):
    return pl.BlockSpec((TILE, width), lambda t: (t, 0))


def whole(*shape):
    return pl.BlockSpec(shape, lambda t: (0,) * len(shape))


def project(x, other, gain, w, cosine, sine, gq, gk, after):
    return call(
        project_body,
        (
            shaped((ROWS, D), BF),
            shaped((ROWS, 256), F32),
            shaped((ROWS, 128), BF),
            shaped((ROWS, 128), BF),
        ),
        grid=(ROWS // TILE,),
        in_specs=halves(D) + [whole(1, D), whole(16, 264, 256), tiles(128), tiles(128), whole(1, 128), whole(1, 128)],
        out_specs=(tiles(D), tiles(256), tiles(128), tiles(128)),
        flops=2 * ROWS * D * 256,
        nbytes=7 * 2**20,
        after=after,
        name="project",
    )(x, other, gain, w, cosine, sine, gq, gk)


def heads_back_body(
    dq_ref, k0_ref, k1_ref, k2_ref, k3_ref, raw_ref, cos_ref, sin_ref, gq_ref, gk_ref, n_ref,
    att_ref, own_ref, other_ref, graw_ref, line_ref, gw_acc, out_acc, head_acc,
):
    step = pl.program_id(0)

    @pl.when(step == 0)
    def _():
        gw_acc[...] = jnp.zeros_like(gw_acc)
        out_acc[...] = jnp.zeros_like(out_acc)
        head_acc[...] = jnp.zeros_like(head_acc)

    cosine, sine = cos_ref[...], sin_ref[...]

    def back(raw, grad, gain):
        r = lax.rsqrt(head_mean(raw * raw) + EPSILON)
        n = raw * r
        up = grad * cosine + swap_halves(grad * sine)
        scaled = up * gain
        return r * (scaled - n * head_mean(scaled * n)), jnp.sum(up * n, axis=0, keepdims=True)

    raw = raw_ref[...]
    graw_q, gain_q = back(raw[:, :128], dq_ref[...], gq_ref[...])
    dkv = (k0_ref[...].astype(F32) + k1_ref[...].astype(F32)) + (
        k2_ref[...].astype(F32) + k3_ref[...].astype(F32)
    )
    graw_k, gain_k = back(raw[:, 128:], dkv, gk_ref[...])
    gain_k = jnp.where(low_half(gain_k.shape), gain_k, 0.0)
    head_acc[...] += jnp.concatenate([gain_q, gain_k], axis=1)
    graw = jnp.concatenate([graw_q, jnp.where(low_half(dkv.shape), graw_k, dkv)], axis=1).astype(BF)
    graw_ref[...] = graw
    gw_acc[...] += dot_rows(n_ref[...], graw)
    out_acc[...] += dot_rows(att_ref[...], picked(own_ref, other_ref))

    @pl.when(step == pl.num_programs(0) - 1)
    def _():
        heads = jnp.broadcast_to(head_acc[...], (8, 256))
        for k in range(16):
            rows = out_acc[8 * k : 8 * k + 8]
            parts = [gw_acc[64 * k : 64 * k + 64], heads]
            parts += [rows[:, c : c + 256] for c in range(0, D, 256)]
            line_ref[k] = jnp.concatenate(parts, axis=0).astype(BF)


def heads_back(dq, dkvs, raw, cosine, sine, gq, gk, normed, att, b_own, b_other, after):
    return call(
        heads_back_body,
        (shaped((ROWS, 256), BF), shaped((16, 104, 256), BF)),
        grid=(ROWS // TILE,),
        in_specs=[tiles(128)] * 5
        + [tiles(256), tiles(128), tiles(128), whole(1, 128), whole(1, 128), tiles(D), tiles(128)]
        + halves(D),
        out_specs=(tiles(256), whole(16, 104, 256)),
        scratch_shapes=[
            pltpu.VMEM((D, 256), F32),
            pltpu.VMEM((128, D), F32),
            pltpu.VMEM((1, 256), F32),
        ],
        flops=2 * ROWS * D * 384,
        nbytes=10 * 2**20,
        after=after,
        name="heads_back",
    )(dq, *dkvs, raw, cosine, sine, gq, gk, normed, att, b_own, b_other)


def rows_back_body(graw_ref, own_ref, other_ref, gain_ref, w_ref, out_own, out_other):
    x = picked(own_ref, other_ref).astype(F32)
    grad = dot_cols(graw_ref[...], w_ref[:, :64].reshape(D, 256))
    part = norm_back(x, gain_ref[...].astype(F32), grad).astype(BF)

    @pl.when(pl.program_id(0) < 2)
    def _():
        out_own[...] = part

    @pl.when(pl.program_id(0) >= 2)
    def _():
        out_other[...] = part


def rows_back(graw, x, other, gain, w, after):
    return call(
        rows_back_body,
        (shaped((ROWS // 2, D), BF),) * 2,
        grid=(ROWS // TILE,),
        in_specs=[tiles(256)] + halves(D) + [whole(1, D), whole(16, 264, 256)],
        out_specs=tuple(halves(D)),
        flops=2 * ROWS * D * 256,
        nbytes=5 * 2**20,
        after=after,
        name="rows_back",
    )(graw, x, other, gain, w)


def stored(tab_ref, ref, half, h):
    return jnp.concatenate(
        [ref[c, tab_ref[4 + 2 * h + zz], half] for c in range(2) for zz in range(2)], axis=0
    )


def store(tab_ref, ref, half, h, block):
    for c in range(2):
        for zz in range(2):
            row = (c * 2 + zz) * 64
            ref[c, tab_ref[4 + 2 * h + zz], half] = block[row : row + 64]


def heads_across(block):
    flat = block.astype(F32).T
    return jnp.concatenate([flat[:HD], flat[HD:]], axis=1)


def diagonal_mask(core):
    def place(t):
        return ((t >> 6) & 1) * 128 + ((t >> 7) ^ core) * 64 + (t & 63)

    keys = place(lax.broadcasted_iota(jnp.int32, (BLK, 2 * BLK), 0))
    queries = place(lax.broadcasted_iota(jnp.int32, (BLK, 2 * BLK), 1) & 255)
    return keys <= queries


def pair_at(tab_ref, i, o):
    count = tab_ref[2 * o]
    first = i < count
    qb = 2 * o + jnp.where(first, 0, 1)
    slot = tab_ref[8 + jnp.where(first, i, i - count)]
    return qb, slot


def attend_body(tab_ref, q_ref, kv0, kv1, kv2, kv3, att_ref, attT_ref, lse_ref, qT, kv, vT, acc):
    zeros = jnp.zeros((HD, 2 * BLK), BF)
    for qb in range(4):
        qT[qb, :HD] = heads_across(stored(tab_ref, q_ref, qb // 2, qb % 2)).astype(BF)
        qT[qb, HD:] = zeros
    for slot in range(16):
        block = stored(tab_ref, (kv0, kv1, kv2, kv3)[slot // 4], (slot >> 1) & 1, slot & 1)
        kv[slot] = block
        flat = block.astype(F32).T
        vT[slot] = jnp.concatenate([jnp.ones((16, BLK), F32), flat[HD:]], axis=0).astype(BF)
    acc[...] = jnp.zeros_like(acc)

    def pair(qb, slot, mask=None):
        p = jnp.exp(dot(kv[slot], qT[qb]))
        if mask is not None:
            p = jnp.where(mask, p, 0.0)
        acc[qb] += dot(vT[slot], p.astype(BF))

    def step(i, carry):
        for o in range(2):
            pair(*pair_at(tab_ref, i, o))
        return carry

    lax.fori_loop(0, 15, step, 0)
    mask = diagonal_mask(tab_ref[24])
    for qb in range(4):
        pair(qb, tab_ref[8 + tab_ref[qb]], mask)
        total = acc[qb, :1]
        out = acc[qb, 16:] / total
        flat = jnp.concatenate([out[:, :BLK], out[:, BLK:]], axis=0)
        attT_ref[qb] = flat
        lse_ref[qb] = jnp.log(total)
        store(tab_ref, att_ref, qb // 2, qb % 2, flat.T.astype(BF))


def in_smem():
    return pl.BlockSpec(memory_space=pltpu.SMEM)


def in_vmem():
    return pl.BlockSpec(memory_space=pltpu.VMEM)


def attend(table, q, kvs, after):
    return call(
        attend_body,
        (
            shaped((2, 4, 2, 64, 128), BF),
            shaped((4, 128, BLK), F32),
            shaped((4, 1, 2 * BLK), F32),
        ),
        in_specs=[in_smem()] + [in_vmem()] * 5,
        out_specs=(in_vmem(), in_vmem(), in_vmem()),
        scratch_shapes=[
            pltpu.VMEM((4, 128, 2 * BLK), BF),
            pltpu.VMEM((16, BLK, 128), BF),
            pltpu.VMEM((16, HD + 16, BLK), BF),
            pltpu.VMEM((4, HD + 16, 2 * BLK), F32),
        ],
        flops=34 * 4 * BLK * 2 * BLK * 128,
        nbytes=2 * 2**20,
        after=after,
        name="attend",
    )(table, q, *kvs)


def attend_back_body(
    tab_ref, q_ref, kv0, kv1, kv2, kv3, g0, g1, g2, g3, attT_ref, lse_ref,
    dq_ref, dkv0, dkv1, dkv2, dkv3, g_ref, qT, gT, qn, gn, kv, kT, delta, dqT, dkv,
):
    for k, ref in enumerate((g0, g1, g2, g3)):
        g_ref[0, k], g_ref[1, k] = ref[0], ref[1]
    zeros = jnp.zeros((HD, 2 * BLK), F32)
    for qb in range(4):
        across = jnp.concatenate([heads_across(stored(tab_ref, q_ref, qb // 2, qb % 2)), zeros], axis=0)
        qT[qb] = across.astype(BF)
        qn[qb] = across.T.astype(BF)
        g_across = heads_across(stored(tab_ref, g_ref, qb // 2, qb % 2))
        out = attT_ref[qb]
        out = jnp.concatenate([out[:HD], out[HD:]], axis=1)
        delta[qb] = jnp.sum(g_across * out, axis=0, keepdims=True)
        g_across = jnp.concatenate([zeros, g_across], axis=0)
        gT[qb] = g_across.astype(BF)
        gn[qb] = g_across.T.astype(BF)
    for slot in range(16):
        block = stored(tab_ref, (kv0, kv1, kv2, kv3)[slot // 4], (slot >> 1) & 1, slot & 1)
        kv[slot] = block
        kT[slot] = block.astype(F32).T[:HD].astype(BF)
    dqT[...] = jnp.zeros_like(dqT)
    dkv[...] = jnp.zeros_like(dkv)

    def pair(qb, slot, mask=None):
        keys = kv[slot]
        p = jnp.exp(dot(keys, qT[qb]) - lse_ref[qb])
        if mask is not None:
            p = jnp.where(mask, p, 0.0)
        ds = (p * (dot(keys, gT[qb]) - delta[qb])).astype(BF)
        dkv[slot] += dot(ds, qn[qb]) + dot(p.astype(BF), gn[qb])
        dqT[qb] += dot(kT[slot], ds)

    def step(i, carry):
        for o in range(2):
            pair(*pair_at(tab_ref, i, o))
        return carry

    lax.fori_loop(0, 15, step, 0)
    mask = diagonal_mask(tab_ref[24])
    for qb in range(4):
        pair(qb, tab_ref[8 + tab_ref[qb]], mask)
        flat = jnp.concatenate([dqT[qb, :, :BLK], dqT[qb, :, BLK:]], axis=0)
        store(tab_ref, dq_ref, qb // 2, qb % 2, flat.T * 0.125)
    for slot in range(16):
        out = (dkv0, dkv1, dkv2, dkv3)[slot // 4]
        store(tab_ref, out, (slot >> 1) & 1, slot & 1, dkv[slot].astype(BF))


def attend_back(table, q, kvs, gs, attT, lse):
    return call(
        attend_back_body,
        (shaped((2, 4, 2, 64, 128), F32),) + (shaped((2, 4, 2, 64, 128), BF),) * 4,
        in_specs=[in_smem()] + [in_vmem()] * 11,
        out_specs=(in_vmem(),) * 5,
        scratch_shapes=[
            pltpu.VMEM((2, 4, 2, 64, 128), BF),
            pltpu.VMEM((4, 128, 2 * BLK), BF),
            pltpu.VMEM((4, 128, 2 * BLK), BF),
            pltpu.VMEM((4, 2 * BLK, 128), BF),
            pltpu.VMEM((4, 2 * BLK, 128), BF),
            pltpu.VMEM((16, BLK, 128), BF),
            pltpu.VMEM((16, HD, BLK), BF),
            pltpu.VMEM((4, 1, 2 * BLK), F32),
            pltpu.VMEM((4, HD, 2 * BLK), F32),
            pltpu.VMEM((16, BLK, 128), F32),
        ],
        flops=34 * 10 * BLK * 2 * BLK * 128,
        nbytes=4 * 2**20,
        name="attend_back",
    )(table, q, *kvs, *gs, attT, lse)


def ffn_body(
    a0, a1, a2, a3, b0, b1, b2, b3, x_own, x_other, g_own, g_other, gain_ref,
    wo_own, wo_other, units_ref, lines_ref,
    mixed_own, mixed_other, part_own, part_other, gw_ref, wo, wgu, wd, gwgu, gwd,
):
    step = pl.program_id(0)

    @pl.when(step == 0)
    def _():
        gwgu[...] = jnp.zeros_like(gwgu)
        gwd[...] = jnp.zeros_like(gwd)
        for k in range(4):
            wo[256 * k : 256 * k + 128] = wo_own[128 * k : 128 * k + 128]
            wo[256 * k + 128 : 256 * k + 256] = wo_other[128 * k : 128 * k + 128]
        wgu[...] = units_ref[...].reshape(D, 2 * FP)
        rows = []
        for k in range(16):
            parts = [lines_ref[k, r : r + 40].astype(F32)[:36] for r in range(104, 264, 40)]
            rows.append(jnp.concatenate(parts, axis=1))
        rows.append(jnp.zeros((FP - FS, D), F32))
        wd[...] = jnp.concatenate(rows, axis=0).astype(BF)

    core, first = step // 2, step % 2 * 2
    pieces = []
    for k, refs in enumerate(((a0, b0), (a1, b1), (a2, b2), (a3, b3))):
        for c, ref in enumerate(refs):
            at = [(core ^ c) * 512 + ((first + j - k) & 3) * 128 for j in range(2)]
            pieces.append(jnp.concatenate([ref[pl.ds(r, 128)] for r in at], axis=0))
    middle = picked(x_own, x_other).astype(F32) + dot(jnp.concatenate(pieces, axis=1), wo[...])
    gain = gain_ref[...].astype(F32)
    normed = (middle * rms_of(middle) * gain).astype(BF)
    pre = dot(normed, wgu[...])
    gate, up = pre[:, :FP], pre[:, FP:]
    s = 1.0 / (1.0 + jnp.exp(-gate))
    act = gate * s
    hidden = (act * up).astype(BF)
    row = lax.broadcasted_iota(jnp.int32, (TILE, 1), 0)
    here = jnp.logical_and(step == 0, row < 128)
    mixed = (dot(hidden, wd[...]) + jnp.where(here, middle, 0.0)).astype(BF)
    g = picked(g_own, g_other)
    gh = dot_cols(g, wd[...])
    gwd[...] += dot_rows(hidden, g)
    gpre = jnp.concatenate([gh * up * s * (1.0 + gate * (1.0 - s)), gh * act], axis=1).astype(BF)
    gwgu[...] += dot_rows(normed, gpre)
    part = norm_back(middle, gain, dot_cols(gpre, wgu[...])).astype(BF)

    @pl.when(step < 2)
    def _():
        mixed_own[...] = mixed
        part_own[...] = part

    @pl.when(step >= 2)
    def _():
        mixed_other[...] = mixed
        part_other[...] = part

    @pl.when(step == pl.num_programs(0) - 1)
    def _():
        for k in range(16):
            gw_ref[k, :64] = gwgu[64 * k : 64 * k + 64].astype(BF)
            rows = jnp.concatenate([gwd[36 * k : 36 * k + 36], jnp.zeros((4, D), F32)], axis=0)
            rows = jnp.concatenate([rows, jnp.zeros((40, 2 * FP - D), F32)], axis=1)
            gw_ref[k, 64:] = rows.astype(BF)


def ffn(own, other, x, g, gain, wo, units, lines):
    return call(
        ffn_body,
        (shaped((ROWS // 2, D), BF),) * 4 + (shaped((16, 104, 2 * FP), BF),),
        grid=(ROWS // TILE,),
        in_specs=[whole(ROWS, 128)] * 8
        + halves(D)
        + halves(D)
        + [whole(1, D), whole(D // 2, D), whole(D // 2, D)]
        + [whole(16, 64, 2 * FP), whole(16, 264, 256)],
        out_specs=tuple(halves(D) * 2) + (whole(16, 104, 2 * FP),),
        scratch_shapes=[
            pltpu.VMEM((D, D), BF),
            pltpu.VMEM((D, 2 * FP), BF),
            pltpu.VMEM((FP, D), BF),
            pltpu.VMEM((D, 2 * FP), F32),
            pltpu.VMEM((FP, D), F32),
        ],
        flops=2 * ROWS * D * (D + 9 * FP),
        nbytes=24 * 2**20,
        name="ffn",
    )(*own, *other, *x, *g, gain, *wo, units, lines)


def branch_body(g_ref, t0, t1, t2, t3, wo_own, wo_other, mid_ref, branch_ref, own_ref, other_ref):
    total = g_ref[...].astype(F32) + t0[...] + t1[...].astype(F32)
    total += t2[...].astype(F32) + t3[...].astype(F32)
    mid_ref[...] = total
    branch = total.astype(BF)
    branch_ref[...] = branch
    for w_ref, out_ref in ((wo_own, own_ref), (wo_other, other_ref)):
        grad = dot_cols(branch, w_ref[...]).astype(BF)
        for k in range(4):
            at = (-k) % 4 * 128
            out_ref[k] = grad[:, at : at + 128]


def branch_of(g_rows, terms, wo):
    return call(
        branch_body,
        (shaped((128, D), F32), shaped((128, D), BF)) + (shaped((4, 128, 128), BF),) * 2,
        in_specs=[in_vmem()] * 7,
        out_specs=(in_vmem(),) * 4,
        flops=2 * 128 * D * D,
        nbytes=4 * 2**20,
        name="branch",
    )(g_rows, *terms, *wo)


def columns_body(wq, wk, wv, wg, wu, gains_ref, out_ref):
    wq, wk, wv, wg, wu = (w[...].astype(F32) for w in (wq, wk, wv, wg, wu))
    gains = jnp.concatenate([gains_ref[...].astype(F32), jnp.zeros((8, 2 * FP), F32)], axis=1)
    gap = jnp.zeros((8, FP - FS), F32)
    for s in range(8):
        parts = [w[:, s * n : s * n + n] for w, n in ((wq, 128), (wk, HD), (wv, HD))]
        parts += [wg[:, s * FS : s * FS + FS], gap, wu[:, s * FS : s * FS + FS], gap]
        out_ref[s] = jnp.concatenate([jnp.concatenate(parts, axis=1), gains], axis=0).astype(BF)


def pack_columns(weights, gains):
    return call(
        columns_body,
        shaped((8, 16, 256 + 2 * FP), BF),
        in_specs=[in_vmem()] * 6,
        out_specs=in_vmem(),
        nbytes=2**20,
        name="pack_columns",
    )(*weights, gains)


def lines_body(cols_ref, downs_ref, out_ref):
    gains = cols_ref[0, :, :256].astype(F32)[8:]
    for s in range(1, 8):
        gains += cols_ref[s, :, :256].astype(F32)[8:]
    downs = downs_ref[...].astype(F32)
    outs, downs = downs[:8], jnp.concatenate([downs[8:], jnp.zeros((4, D), F32)], axis=0)
    parts = [cols_ref[s, :, :256].astype(F32)[:8] for s in range(8)] + [gains]
    parts += [outs[:, c : c + 256] for c in range(0, D, 256)]
    parts += [downs[:, c : c + 256] for c in range(0, D, 256)]
    line = jnp.concatenate(parts, axis=0).astype(BF)
    for k in range(16):
        out_ref[k] = line


def pack_lines(cols, downs):
    return call(
        lines_body,
        shaped((16, 264, 256), BF),
        in_specs=[in_vmem()] * 2,
        out_specs=in_vmem(),
        nbytes=3 * 2**20,
        name="pack_lines",
    )(cols, downs)


def units_body(cols_ref, out_ref):
    rows = [cols_ref[s, :, 256:].astype(F32)[:8] for s in range(8)]
    unit = jnp.concatenate(rows, axis=0).astype(BF)
    for k in range(16):
        out_ref[k] = unit


def pack_units(cols):
    return call(
        units_body,
        shaped((16, 64, 2 * FP), BF),
        in_specs=[in_vmem()],
        out_specs=in_vmem(),
        nbytes=3 * 2**20,
        name="pack_units",
    )(cols)


def sum_units_body(in_ref, cols_ref, down_ref):
    total = in_ref[0].astype(F32)
    for k in range(1, 16):
        total += in_ref[k].astype(F32)
    cols_ref[...] = total[:64]
    down_ref[...] = total[64:100, :D]


def sum_units(terms):
    return call(
        sum_units_body,
        (shaped((64, 2 * FP), F32), shaped((36, D), F32)),
        in_specs=[in_vmem()],
        out_specs=(in_vmem(),) * 2,
        nbytes=5 * 2**20,
        name="sum_units",
    )(terms)


def grads_body(lines_ref, units_ref, out_ref):
    heads = jnp.concatenate([lines_ref[64:72], jnp.zeros((8, 2 * FP), F32)], axis=1)
    for s in range(8):
        rows = slice(8 * s, 8 * s + 8)
        grads = jnp.concatenate([lines_ref[rows], units_ref[rows]], axis=1)
        out_ref[s] = jnp.concatenate([grads, heads], axis=0).astype(BF)


def pack_grads(lines, units):
    return call(
        grads_body,
        shaped((8, 16, 256 + 2 * FP), BF),
        in_specs=[in_vmem()] * 2,
        out_specs=in_vmem(),
        nbytes=2**20,
        name="pack_grads",
    )(lines, units)


def unpack_body(
    in_ref, wq, wk, wv, wg, wu, gain_attn, gain_ffn,
    gq_ref, gk_ref, gv_ref, gg_ref, gu_ref, attn_ref, ffn_ref, head_ref,
):
    blocks = [in_ref[s].astype(F32) for s in range(8)]

    def taken(w_ref, g_ref, at, n):
        grad = jnp.concatenate([b[:8, at : at + n] for b in blocks], axis=1)
        g_ref[...] = grad
        return jnp.sum(w_ref[...].astype(F32) * grad, axis=1, keepdims=True)

    attn = taken(wq, gq_ref, 0, 128) + taken(wk, gk_ref, 128, HD) + taken(wv, gv_ref, 192, HD)
    attn_ref[...] = attn / gain_attn[...].astype(F32)
    feed = taken(wg, gg_ref, 256, FS) + taken(wu, gu_ref, 256 + FP, FS)
    ffn_ref[...] = feed / gain_ffn[...].astype(F32)
    heads = blocks[0][8:, :256]
    for b in blocks[1:]:
        heads += b[8:, :256]
    head_ref[...] = heads


def unpack_grads(cols, weights, gains):
    return call(
        unpack_body,
        tuple(shaped(w.shape, F32) for w in weights)
        + (shaped((8, 1), F32), shaped((8, 1), F32), shaped((8, 256), F32)),
        in_specs=[in_vmem()] * 8,
        out_specs=(in_vmem(),) * 8,
        nbytes=2**20,
        name="unpack_grads",
    )(cols, *weights, *gains)


def on_device(
    tokens, cotangent, block_of, attn_gain, ffn_gain, head_gains,
    w_query, w_key, w_value, w_out, w_gate, w_up, w_down,
):
    core, level = lax.axis_index("sp_1"), lax.axis_index("sp_0")
    cycle, half = lax.axis_index("cp_1"), lax.axis_index("cp_0")
    gains_f = head_gains.astype(F32)
    gq = jnp.tile(gains_f[0], 2)[None]
    gk = jnp.tile(gains_f[1], 2)[None]
    cosine, sine, table = row_tables(block_of, core, half, cycle, level)

    place = jnp.arange(8)[:, None] == lax.axis_index(SP)
    gains = jnp.stack([attn_gain, ffn_gain])[:, None, :]
    gains = jnp.where(place[None], gains, jnp.zeros((), BF)).reshape(1, 128)
    gains = jnp.pad(gains, ((0, 7), (0, 128)))
    cols = exchange(pack_columns((w_query, w_key, w_value, w_gate, w_up), gains), SP)
    rows = own_first(jnp.stack([tokens, cotangent], axis=1), half)
    rows = jnp.stack([rows[0], pair(rows[1], "cp_0")], axis=1).reshape(2, 128, D)
    perm = [(d, (d % 16) * 8 + d // 16) for d in range(128)]
    downs = lax.ppermute(jnp.concatenate([w_out, w_down], axis=0), DP_CP_SP, perm)
    line = pack_lines(cols, downs)
    lines = exchange(line, DC)
    gains = lines[:, 64, :128]
    gain_attn, gain_ffn = gains[:, :64].reshape(1, D), gains[:, 64:].reshape(1, D)

    both = around(after(rows, line).reshape(256, D), "sp_0")
    x_own = jnp.concatenate([a[:128] for a in both], axis=0)
    g_own = jnp.concatenate([a[128:] for a in both], axis=0)
    x_other = sibling(x_own)
    g_rows = rows[1]

    units = pack_units(after(cols, line))
    normed, raw, q, kv = project(
        x_own, x_other, gain_attn, lines, cosine, sine, gq, gk, (units,)
    )
    kvs = around(kv, "cp_1")
    units = exchange(after(units, *kvs[1:]), DC)
    g_other = sibling(after(g_own, q))
    wo_rows = jnp.concatenate([lines[:, r : r + 8] for r in range(72, 104, 8)], axis=2)
    wo_own = jnp.concatenate(around(after(wo_rows, *kvs[1:]).reshape(128, D), "sp_0"), axis=0)
    kvs = [a.reshape(2, 4, 2, 64, 128) for a in kvs]
    q = q.reshape(2, 4, 2, 64, 128)
    att, attT, lse = attend(table, q, kvs, ())
    att = att.reshape(ROWS, 128)
    wo = (wo_own, sibling(after(wo_own, att)))
    own = around(att, "sp_0")
    other = [sibling(a) for a in own]
    mixed_own, mixed_other, part_own, part_other, gw_units = ffn(
        own, other, (x_own, x_other), (g_own, g_other), gain_ffn, wo, units, lines
    )

    mids = sum_cores(part_own, part_other)
    terms = [ring(mids[k].astype(BF), "sp_0", 4 - k) for k in (1, 2, 3)]
    gw_units = exchange(gw_units, DC)
    mids = mids[:1] + terms
    grad_middle, branch, for_own, for_other = branch_of(g_rows, mids, wo)
    mixes = sum_cores(mixed_own, after(mixed_other, mids[0]))
    mixes = mixes[:1] + [a.astype(BF) for a in mixes[1:]]
    grad_att = jnp.stack([for_own, sibling(for_other)], axis=1)
    grad_att, *mixes = lax.optimization_barrier((grad_att, *mixes))
    grad_att = [grad_att[0]] + [ring(grad_att[k], "sp_0", k) for k in (1, 2, 3)]
    branch, *mixes = after((branch, *mixes), *grad_att)
    came = [ring(jnp.concatenate([branch, mixes[k]], axis=0), "sp_0", 4 - k) for k in (1, 2, 3)]
    dq, *dkvs = attend_back(
        table, q, kvs, [a.reshape(2, 2, 64, 128) for a in grad_att], attT, lse
    )
    dkvs = [a.reshape(ROWS, 128) for a in dkvs]
    dkvs = dkvs[:1] + [ring(dkvs[k], "cp_1", 4 - k) for k in (1, 2, 3)]
    came = after(came, *dkvs[1:])
    b_own = jnp.concatenate([branch] + [came[k][:128] for k in (2, 1, 0)], axis=0)
    b_other = sibling(b_own)
    mixed = mixes[0] + sum(a[128:].astype(F32) for a in came)
    gw_cols, gw_down = sum_units(gw_units)
    graw, line = heads_back(
        dq.reshape(ROWS, 128), dkvs, raw, cosine, sine, gq, gk, normed, att, b_own, b_other,
        (gw_cols,),
    )
    terms = jnp.sum(exchange(line, DC).astype(F32), axis=0)
    lasts = sum_cores(*rows_back(graw, x_own, x_other, gain_attn, lines, ()))
    lasts = [lasts[0]] + [a.astype(BF) for a in lasts[1:]]
    last = grad_middle + lasts[0]
    for k in (1, 2, 3):
        last += ring(lasts[k], "sp_0", 4 - k).astype(F32)
    last = jnp.stack([last, mixed]).astype(BF).reshape(2, 2, 64, D).swapaxes(0, 1)
    rows = own_first(jnp.stack([last[0], pair(last[1], "cp_0")]), half)
    grad_tokens, mixed = rows[:, 0], rows[:, 1]

    back = [(d, s) for s, d in perm]
    cols = exchange(pack_grads(after(terms, last), gw_cols), SP)
    gw_out = jnp.concatenate([terms[r : r + 8] for r in range(72, 104, 8)], axis=1)
    downs = lax.ppermute(jnp.concatenate([gw_out, gw_down], axis=0), DP_CP_SP, back)
    downs = after(downs, cols)
    grad_w_out, grad_w_down = downs[:8], downs[8:]
    weights = (w_query, w_key, w_value, w_gate, w_up)
    gains = (attn_gain[:, None], ffn_gain[:, None])
    *grads, grad_attn_gain, grad_ffn_gain, heads = unpack_grads(cols, weights, gains)
    grad_w_query, grad_w_key, grad_w_value, grad_w_gate, grad_w_up = grads
    heads = heads[0].reshape(4, HD)
    return (
        mixed,
        grad_tokens,
        grad_attn_gain[:, 0],
        grad_ffn_gain[:, 0],
        jnp.stack([heads[0] + heads[1], heads[2]]),
        grad_w_query,
        grad_w_key,
        grad_w_value,
        grad_w_out,
        grad_w_gate,
        grad_w_up,
        grad_w_down,
    )


def solution(mesh):
    torus = Mesh(
        mesh.devices.reshape(mesh.shape["dp"], 2, 4, 4, 2), ("dp", "cp_0", "cp_1", "sp_0", "sp_1")
    )
    rows, split = P("dp", CP_SP, None), P(DP_CP_SP, None)
    in_specs = (rows, rows, P(), P(DP_CP_SP), P(DP_CP_SP), P()) + (split,) * 7
    out_specs = (rows, rows, P(DP_CP_SP), P(DP_CP_SP), P()) + (split,) * 7
    return jax.shard_map(
        on_device, mesh=torus, in_specs=in_specs, out_specs=out_specs, check_vma=False
    )
```

```python
from functools import partial

import jax
import jax.numpy as jnp
from jax import lax
from jax.experimental import pallas as pl
from jax.experimental.pallas import tpu as pltpu
from jax.sharding import Mesh
from jax.sharding import PartitionSpec as P

SP = ("sp_0", "sp_1")
DC = ("dp", "cp_0", "cp_1")
DP_CP_SP = ("dp", "cp_0", "cp_1", "sp_0", "sp_1")
CP_SP = ("cp_0", "cp_1", "sp_0", "sp_1")

EPSILON = 1e-05
ROPE_BASE = 1000000.0
BF = jnp.bfloat16
F32 = jnp.float32

D = 1024
HD = 64
FF = 4608
FS = FF // 8
FP = 640
BLK = 256
ROWS = 1024
TILE = 256
VMEM_LIMIT = 56 * 1024 * 1024


def dot(left, right):
    return jnp.dot(left, right, preferred_element_type=F32)


def dot_rows(left, right):
    return lax.dot_general(left, right, (((0,), (0,)), ((), ())), preferred_element_type=F32)


def dot_cols(left, right):
    return lax.dot_general(left, right, (((1,), (1,)), ((), ())), preferred_element_type=F32)


def call(body, out, **kw):
    flops = kw.pop("flops", 0)
    nbytes = kw.pop("nbytes", 0)
    after = kw.pop("after", ())
    if after:
        inner, count = body, len(after)
        kw["in_specs"] = [pl.BlockSpec(memory_space=pl.ANY)] * count + list(kw["in_specs"])

        def body(*refs):
            return inner(*refs[count:])

        return partial(call(body, out, flops=flops, nbytes=nbytes, **kw), *after)
    return pl.pallas_call(
        body,
        out_shape=out,
        compiler_params=pltpu.CompilerParams(vmem_limit_bytes=VMEM_LIMIT),
        cost_estimate=pl.CostEstimate(flops=flops, bytes_accessed=nbytes, transcendentals=0),
        **kw,
    )


def shaped(shape, dtype):
    return jax.ShapeDtypeStruct(shape, dtype)


def ring(x, axis, k):
    return lax.ppermute(x, axis, [(i, (i + k) % 4) for i in range(4)])


def pair(x, axis):
    return lax.ppermute(x, axis, [(0, 1), (1, 0)])


def sibling(x):
    return pair(x, "sp_1")


def exchange(x, axis):
    return lax.all_to_all(x, axis, 0, 0, tiled=True)


def after(x, *first):
    return lax.optimization_barrier((x, *first))[0]


def around(x, axis):
    return [x] + [ring(x, axis, k) for k in (1, 2, 3)]


def own_first(both, half):
    return jnp.where(half == 0, both, both[::-1])


def swapped(rows):
    return jnp.concatenate([rows[0], pair(rows[1], "cp_0")], axis=0)


def sum_cores(own, other):
    came = sibling(other)
    return [
        own[r : r + 128].astype(F32) + came[r : r + 128].astype(F32) for r in range(0, 512, 128)
    ]


def rms_of(x):
    return lax.rsqrt(jnp.mean(x * x, axis=-1, keepdims=True) + EPSILON)


def norm_back(x, gain, upstream):
    r = rms_of(x)
    n = x * r
    scaled = upstream * gain
    return r * (scaled - n * jnp.mean(scaled * n, axis=-1, keepdims=True))


def low_half(shape):
    return lax.broadcasted_iota(jnp.int32, shape, 1) < HD


def head_mean(v):
    low = low_half(v.shape)
    first = jnp.sum(jnp.where(low, v, 0.0), axis=1, keepdims=True)
    second = jnp.sum(jnp.where(low, 0.0, v), axis=1, keepdims=True)
    return jnp.where(low, first, second) * (1.0 / HD)


def swap_halves(v):
    lane = lax.broadcasted_iota(jnp.int32, v.shape, 1)
    return jnp.where(lane % HD < HD // 2, pltpu.roll(v, 96, 1), pltpu.roll(v, 32, 1))


def row_tables(block_of, core, half, cycle, level):
    slots = jnp.arange(16, dtype=jnp.int32)
    blocks = block_of.reshape(2, 4, 2)
    blocks = jnp.where(half == 0, blocks, blocks[::-1])
    local = lax.dynamic_index_in_dim(blocks, cycle, 1, keepdims=False)
    z = (level - jnp.arange(4, dtype=jnp.int32)) % 4
    pick = (z // 2)[None, :] == 1
    by_z = jnp.where(pick, local[:, 1:], local[:, :1]).T
    entries = HD // 2
    inverse = ROPE_BASE ** (-(2.0 * jnp.arange(entries, dtype=F32)) / HD)
    inverse = jnp.tile(inverse, 4)
    sign = jnp.tile(jnp.concatenate([-jnp.ones(entries, F32), jnp.ones(entries, F32)]), 2)
    first = (by_z.reshape(8) * BLK).astype(F32)[:, None] * inverse[None]
    rel = jnp.arange(2, dtype=jnp.int32)[:, None, None]
    row = jnp.arange(64, dtype=jnp.int32)[None, None, :]
    inner = ((z % 2)[None, :, None] * 128 + (rel ^ core) * 64 + row).reshape(512)
    inner = inner.astype(F32)[:, None] * inverse[None]
    ca, sa = (f(first).reshape(1, 4, 2, 1, 128) for f in (jnp.cos, jnp.sin))
    cb, sb = (f(inner).reshape(2, 4, 1, 64, 128) for f in (jnp.cos, jnp.sin))
    cosine = (ca * cb - sa * sb).reshape(ROWS, 128)
    sine = ((sa * cb + ca * sb) * sign).reshape(ROWS, 128)
    distance = (cycle - (slots >> 1)) & 3
    at = distance * 4 + ((slots >> 3) ^ half) * 2 + (slots & 1)
    slot_at = jnp.sum(jnp.where(block_of[None, :] == slots[:, None], at[None, :], 0), axis=1)
    place = (level - jnp.arange(4, dtype=jnp.int32)) & 3
    table = jnp.concatenate([local.reshape(4), place, slot_at, core[None]]).astype(jnp.int32)
    return cosine, sine, table


def project_body(own_ref, other_ref, gain_ref, w_ref, cos_ref, sin_ref, gq_ref, gk_ref, n_ref, raw_ref, q_ref, kv_ref):
    x = picked(own_ref, other_ref).astype(F32)
    normed = (x * rms_of(x) * gain_ref[...].astype(F32)).astype(BF)
    n_ref[...] = normed
    raw = dot(normed, w_ref[:, :64].reshape(D, 256))
    raw_ref[...] = raw
    cosine, sine = cos_ref[...], sin_ref[...]

    def turned(v, gain):
        v = v * lax.rsqrt(head_mean(v * v) + EPSILON) * gain
        return (v * cosine + swap_halves(v) * sine).astype(BF)

    q_ref[...] = turned(raw[:, :128], gq_ref[...]) * jnp.asarray(0.125, BF)
    right = raw[:, 128:]
    kv_ref[...] = jnp.where(low_half(right.shape), turned(right, gk_ref[...]), right.astype(BF))


def picked(own_ref, other_ref):
    return jnp.where(pl.program_id(0) < 2, own_ref[...], other_ref[...])


def halves(width):
    return [
        pl.BlockSpec((TILE, width), lambda t: (jnp.minimum(t, 1), 0)),
        pl.BlockSpec((TILE, width), lambda t: (jnp.maximum(t - 2, 0), 0)),
    ]


def tiles(width):
    return pl.BlockSpec((TILE, width), lambda t: (t, 0))


def whole(*shape):
    return pl.BlockSpec(shape, lambda t: (0,) * len(shape))


def project(x, other, gain, w, cosine, sine, gq, gk, after):
    return call(
        project_body,
        (
            shaped((ROWS, D), BF),
            shaped((ROWS, 256), F32),
            shaped((ROWS, 128), BF),
            shaped((ROWS, 128), BF),
        ),
        grid=(ROWS // TILE,),
        in_specs=halves(D) + [whole(1, D), whole(16, 264, 256), tiles(128), tiles(128), whole(1, 128), whole(1, 128)],
        out_specs=(tiles(D), tiles(256), tiles(128), tiles(128)),
        flops=2 * ROWS * D * 256,
        nbytes=7 * 2**20,
        after=after,
        name="project",
    )(x, other, gain, w, cosine, sine, gq, gk)


def heads_back_body(
    dq_ref, k0_ref, k1_ref, k2_ref, k3_ref, raw_ref, cos_ref, sin_ref, gq_ref, gk_ref, n_ref,
    att_ref, own_ref, other_ref, graw_ref, line_ref, gw_acc, out_acc, head_acc,
):
    step = pl.program_id(0)

    @pl.when(step == 0)
    def _():
        gw_acc[...] = jnp.zeros_like(gw_acc)
        out_acc[...] = jnp.zeros_like(out_acc)
        head_acc[...] = jnp.zeros_like(head_acc)

    cosine, sine = cos_ref[...], sin_ref[...]

    def back(raw, grad, gain):
        r = lax.rsqrt(head_mean(raw * raw) + EPSILON)
        n = raw * r
        up = grad * cosine + swap_halves(grad * sine)
        scaled = up * gain
        return r * (scaled - n * head_mean(scaled * n)), jnp.sum(up * n, axis=0, keepdims=True)

    raw = raw_ref[...]
    graw_q, gain_q = back(raw[:, :128], dq_ref[...], gq_ref[...])
    dkv = (k0_ref[...].astype(F32) + k1_ref[...].astype(F32)) + (
        k2_ref[...].astype(F32) + k3_ref[...].astype(F32)
    )
    graw_k, gain_k = back(raw[:, 128:], dkv, gk_ref[...])
    gain_k = jnp.where(low_half(gain_k.shape), gain_k, 0.0)
    head_acc[...] += jnp.concatenate([gain_q, gain_k], axis=1)
    graw = jnp.concatenate([graw_q, jnp.where(low_half(dkv.shape), graw_k, dkv)], axis=1).astype(BF)
    graw_ref[...] = graw
    gw_acc[...] += dot_rows(n_ref[...], graw)
    out_acc[...] += dot_rows(att_ref[...], picked(own_ref, other_ref))

    @pl.when(step == pl.num_programs(0) - 1)
    def _():
        heads = jnp.broadcast_to(head_acc[...], (8, 256))
        for k in range(16):
            rows = out_acc[8 * k : 8 * k + 8]
            parts = [gw_acc[64 * k : 64 * k + 64], heads]
            parts += [rows[:, c : c + 256] for c in range(0, D, 256)]
            line_ref[k] = jnp.concatenate(parts, axis=0).astype(BF)


def heads_back(dq, dkvs, raw, cosine, sine, gq, gk, normed, att, b_own, b_other, after):
    return call(
        heads_back_body,
        (shaped((ROWS, 256), BF), shaped((16, 104, 256), BF)),
        grid=(ROWS // TILE,),
        in_specs=[tiles(128)] * 5
        + [tiles(256), tiles(128), tiles(128), whole(1, 128), whole(1, 128), tiles(D), tiles(128)]
        + halves(D),
        out_specs=(tiles(256), whole(16, 104, 256)),
        scratch_shapes=[
            pltpu.VMEM((D, 256), F32),
            pltpu.VMEM((128, D), F32),
            pltpu.VMEM((1, 256), F32),
        ],
        flops=2 * ROWS * D * 384,
        nbytes=10 * 2**20,
        after=after,
        name="heads_back",
    )(dq, *dkvs, raw, cosine, sine, gq, gk, normed, att, b_own, b_other)


def rows_back_body(graw_ref, own_ref, other_ref, gain_ref, w_ref, out_own, out_other):
    x = picked(own_ref, other_ref).astype(F32)
    grad = dot_cols(graw_ref[...], w_ref[:, :64].reshape(D, 256))
    part = norm_back(x, gain_ref[...].astype(F32), grad).astype(BF)

    @pl.when(pl.program_id(0) < 2)
    def _():
        out_own[...] = part

    @pl.when(pl.program_id(0) >= 2)
    def _():
        out_other[...] = part


def rows_back(graw, x, other, gain, w, after):
    return call(
        rows_back_body,
        (shaped((ROWS // 2, D), BF),) * 2,
        grid=(ROWS // TILE,),
        in_specs=[tiles(256)] + halves(D) + [whole(1, D), whole(16, 264, 256)],
        out_specs=tuple(halves(D)),
        flops=2 * ROWS * D * 256,
        nbytes=5 * 2**20,
        after=after,
        name="rows_back",
    )(graw, x, other, gain, w)


def stored(tab_ref, ref, half, h):
    return jnp.concatenate(
        [ref[c, tab_ref[4 + 2 * h + zz], half] for c in range(2) for zz in range(2)], axis=0
    )


def store(tab_ref, ref, half, h, block):
    for c in range(2):
        for zz in range(2):
            row = (c * 2 + zz) * 64
            ref[c, tab_ref[4 + 2 * h + zz], half] = block[row : row + 64]


def heads_across(block):
    flat = block.astype(F32).T
    return jnp.concatenate([flat[:HD], flat[HD:]], axis=1)


def diagonal_mask(core):
    def place(t):
        return ((t >> 6) & 1) * 128 + ((t >> 7) ^ core) * 64 + (t & 63)

    keys = place(lax.broadcasted_iota(jnp.int32, (BLK, 2 * BLK), 0))
    queries = place(lax.broadcasted_iota(jnp.int32, (BLK, 2 * BLK), 1) & 255)
    return keys <= queries


def pair_at(tab_ref, i, o):
    count = tab_ref[2 * o]
    first = i < count
    qb = 2 * o + jnp.where(first, 0, 1)
    slot = tab_ref[8 + jnp.where(first, i, i - count)]
    return qb, slot


def attend_body(tab_ref, q_ref, kv0, kv1, kv2, kv3, att_ref, attT_ref, lse_ref, qT, kv, vT, acc):
    zeros = jnp.zeros((HD, 2 * BLK), BF)
    for qb in range(4):
        qT[qb, :HD] = heads_across(stored(tab_ref, q_ref, qb // 2, qb % 2)).astype(BF)
        qT[qb, HD:] = zeros
    for slot in range(16):
        block = stored(tab_ref, (kv0, kv1, kv2, kv3)[slot // 4], (slot >> 1) & 1, slot & 1)
        kv[slot] = block
        flat = block.astype(F32).T
        vT[slot] = jnp.concatenate([jnp.ones((16, BLK), F32), flat[HD:]], axis=0).astype(BF)
    acc[...] = jnp.zeros_like(acc)

    def pair(qb, slot, mask=None):
        p = jnp.exp(dot(kv[slot], qT[qb]))
        if mask is not None:
            p = jnp.where(mask, p, 0.0)
        acc[qb] += dot(vT[slot], p.astype(BF))

    def step(i, carry):
        for o in range(2):
            pair(*pair_at(tab_ref, i, o))
        return carry

    lax.fori_loop(0, 15, step, 0, unroll=15)
    mask = diagonal_mask(tab_ref[24])
    for qb in range(4):
        pair(qb, tab_ref[8 + tab_ref[qb]], mask)
        total = acc[qb, :1]
        out = acc[qb, 16:] / total
        flat = jnp.concatenate([out[:, :BLK], out[:, BLK:]], axis=0)
        attT_ref[qb] = flat
        lse_ref[qb] = jnp.log(total)
        store(tab_ref, att_ref, qb // 2, qb % 2, flat.T.astype(BF))


def in_smem():
    return pl.BlockSpec(memory_space=pltpu.SMEM)


def in_vmem():
    return pl.BlockSpec(memory_space=pltpu.VMEM)


def attend(table, q, kvs, after):
    return call(
        attend_body,
        (
            shaped((2, 4, 2, 64, 128), BF),
            shaped((4, 128, BLK), F32),
            shaped((4, 1, 2 * BLK), F32),
        ),
        in_specs=[in_smem()] + [in_vmem()] * 5,
        out_specs=(in_vmem(), in_vmem(), in_vmem()),
        scratch_shapes=[
            pltpu.VMEM((4, 128, 2 * BLK), BF),
            pltpu.VMEM((16, BLK, 128), BF),
            pltpu.VMEM((16, HD + 16, BLK), BF),
            pltpu.VMEM((4, HD + 16, 2 * BLK), F32),
        ],
        flops=34 * 4 * BLK * 2 * BLK * 128,
        nbytes=2 * 2**20,
        after=after,
        name="attend",
    )(table, q, *kvs)


def attend_back_body(
    tab_ref, q_ref, kv0, kv1, kv2, kv3, g0, g1, g2, g3, attT_ref, lse_ref,
    dq_ref, dkv0, dkv1, dkv2, dkv3, g_ref, qT, gT, qn, gn, kv, kT, delta, dqT, dkv,
):
    for k, ref in enumerate((g0, g1, g2, g3)):
        g_ref[0, k], g_ref[1, k] = ref[0], ref[1]
    zeros = jnp.zeros((HD, 2 * BLK), F32)
    for qb in range(4):
        across = jnp.concatenate([heads_across(stored(tab_ref, q_ref, qb // 2, qb % 2)), zeros], axis=0)
        qT[qb] = across.astype(BF)
        qn[qb] = across.T.astype(BF)
        g_across = heads_across(stored(tab_ref, g_ref, qb // 2, qb % 2))
        out = attT_ref[qb]
        out = jnp.concatenate([out[:HD], out[HD:]], axis=1)
        delta[qb] = jnp.sum(g_across * out, axis=0, keepdims=True)
        g_across = jnp.concatenate([zeros, g_across], axis=0)
        gT[qb] = g_across.astype(BF)
        gn[qb] = g_across.T.astype(BF)
    for slot in range(16):
        block = stored(tab_ref, (kv0, kv1, kv2, kv3)[slot // 4], (slot >> 1) & 1, slot & 1)
        kv[slot] = block
        kT[slot] = block.astype(F32).T[:HD].astype(BF)
    dqT[...] = jnp.zeros_like(dqT)
    dkv[...] = jnp.zeros_like(dkv)

    def pair(qb, slot, mask=None):
        keys = kv[slot]
        p = jnp.exp(dot(keys, qT[qb]) - lse_ref[qb])
        if mask is not None:
            p = jnp.where(mask, p, 0.0)
        ds = (p * (dot(keys, gT[qb]) - delta[qb])).astype(BF)
        dkv[slot] += dot(ds, qn[qb]) + dot(p.astype(BF), gn[qb])
        dqT[qb] += dot(kT[slot], ds)

    def step(i, carry):
        for o in range(2):
            pair(*pair_at(tab_ref, i, o))
        return carry

    lax.fori_loop(0, 15, step, 0, unroll=15)
    mask = diagonal_mask(tab_ref[24])
    for qb in range(4):
        pair(qb, tab_ref[8 + tab_ref[qb]], mask)
        flat = jnp.concatenate([dqT[qb, :, :BLK], dqT[qb, :, BLK:]], axis=0)
        store(tab_ref, dq_ref, qb // 2, qb % 2, flat.T * 0.125)
    for slot in range(16):
        out = (dkv0, dkv1, dkv2, dkv3)[slot // 4]
        store(tab_ref, out, (slot >> 1) & 1, slot & 1, dkv[slot].astype(BF))


def attend_back(table, q, kvs, gs, attT, lse):
    return call(
        attend_back_body,
        (shaped((2, 4, 2, 64, 128), F32),) + (shaped((2, 4, 2, 64, 128), BF),) * 4,
        in_specs=[in_smem()] + [in_vmem()] * 11,
        out_specs=(in_vmem(),) * 5,
        scratch_shapes=[
            pltpu.VMEM((2, 4, 2, 64, 128), BF),
            pltpu.VMEM((4, 128, 2 * BLK), BF),
            pltpu.VMEM((4, 128, 2 * BLK), BF),
            pltpu.VMEM((4, 2 * BLK, 128), BF),
            pltpu.VMEM((4, 2 * BLK, 128), BF),
            pltpu.VMEM((16, BLK, 128), BF),
            pltpu.VMEM((16, HD, BLK), BF),
            pltpu.VMEM((4, 1, 2 * BLK), F32),
            pltpu.VMEM((4, HD, 2 * BLK), F32),
            pltpu.VMEM((16, BLK, 128), F32),
        ],
        flops=34 * 10 * BLK * 2 * BLK * 128,
        nbytes=4 * 2**20,
        name="attend_back",
    )(table, q, *kvs, *gs, attT, lse)


def ffn_body(
    a0, a1, a2, a3, b0, b1, b2, b3, x_own, x_other, g_own, g_other, gain_ref,
    wo_own, wo_other, units_ref, lines_ref,
    mixed_own, mixed_other, part_own, part_other, gw_ref, wd, n_all, p_all, h_all,
):
    step = pl.program_id(0)

    @pl.when(step == 0)
    def _():
        rows = []
        for k in range(16):
            parts = [lines_ref[k, r : r + 40].astype(F32)[:36] for r in range(104, 264, 40)]
            rows.append(jnp.concatenate(parts, axis=1))
        rows.append(jnp.zeros((FP - FS, D), F32))
        wd[...] = jnp.concatenate(rows, axis=0).astype(BF)

    core, first = step // 2, step % 2 * 2
    middle = picked(x_own, x_other).astype(F32)
    for c, (refs, w_ref) in enumerate((((a0, a1, a2, a3), wo_own), ((b0, b1, b2, b3), wo_other))):
        pieces = []
        for k, ref in enumerate(refs):
            at = [(core ^ c) * 512 + ((first + j - k) & 3) * 128 for j in range(2)]
            pieces.append(jnp.concatenate([ref[pl.ds(r, 128)] for r in at], axis=0))
        middle += dot(jnp.concatenate(pieces, axis=1), w_ref[...])
    gain = gain_ref[...].astype(F32)
    normed = (middle * rms_of(middle) * gain).astype(BF)
    wgu = units_ref[...].reshape(D, 2 * FP)
    pre = dot(normed, wgu)
    gate, up = pre[:, :FP], pre[:, FP:]
    s = 1.0 / (1.0 + jnp.exp(-gate))
    act = gate * s
    hidden = (act * up).astype(BF)
    row = lax.broadcasted_iota(jnp.int32, (TILE, 1), 0)
    here = jnp.logical_and(step == 0, row < 128)
    mixed = (dot(hidden, wd[...]) + jnp.where(here, middle, 0.0)).astype(BF)
    r = pl.ds(pl.multiple_of(step % 2 * TILE, TILE), TILE)
    g = jnp.where(step < 2, g_own[r], g_other[r])
    gh = dot_cols(g, wd[...])
    at = pl.ds(pl.multiple_of(step * TILE, TILE), TILE)
    h_all[at], n_all[at] = hidden, normed
    gpre = jnp.concatenate([gh * up * s * (1.0 + gate * (1.0 - s)), gh * act], axis=1).astype(BF)
    p_all[at] = gpre
    part = norm_back(middle, gain, dot_cols(gpre, wgu)).astype(BF)

    @pl.when(step < 2)
    def _():
        mixed_own[...] = mixed
        part_own[...] = part

    @pl.when(step >= 2)
    def _():
        mixed_other[...] = mixed
        part_other[...] = part

    @pl.when(step == pl.num_programs(0) - 1)
    def _():
        for k in range(4):
            cols = dot_rows(n_all[:, 256 * k : 256 * k + 256], p_all[...])
            for j in range(4):
                gw_ref[4 * k + j, :64] = cols[64 * j : 64 * j + 64].astype(BF)
        h = h_all[...]
        downs = dot_rows(h[:512], g_own[...]) + dot_rows(h[512:], g_other[...])
        for k in range(16):
            rows = jnp.concatenate([downs[36 * k : 36 * k + 36], jnp.zeros((4, D), F32)], axis=0)
            rows = jnp.concatenate([rows, jnp.zeros((40, 2 * FP - D), F32)], axis=1)
            gw_ref[k, 64:] = rows.astype(BF)


def ffn(own, other, x, g, gain, wo, units, lines):
    return call(
        ffn_body,
        (shaped((ROWS // 2, D), BF),) * 4 + (shaped((16, 104, 2 * FP), BF),),
        grid=(ROWS // TILE,),
        in_specs=[whole(ROWS, 128)] * 8
        + halves(D)
        + [whole(ROWS // 2, D)] * 2
        + [whole(1, D), whole(D // 2, D), whole(D // 2, D)]
        + [whole(16, 64, 2 * FP), whole(16, 264, 256)],
        out_specs=tuple(halves(D) * 2) + (whole(16, 104, 2 * FP),),
        scratch_shapes=[
            pltpu.VMEM((FP, D), BF),
            pltpu.VMEM((ROWS, D), BF),
            pltpu.VMEM((ROWS, 2 * FP), BF),
            pltpu.VMEM((ROWS, FP), BF),
        ],
        flops=2 * ROWS * D * (D + 9 * FP),
        nbytes=24 * 2**20,
        name="ffn",
    )(*own, *other, *x, *g, gain, *wo, units, lines)


def branch_body(g_ref, t0, t1, t2, t3, wo_own, wo_other, mid_ref, branch_ref, own_ref, other_ref):
    total = g_ref[...].astype(F32) + t0[...] + t1[...].astype(F32)
    total += t2[...].astype(F32) + t3[...].astype(F32)
    mid_ref[...] = total
    branch = total.astype(BF)
    branch_ref[...] = branch
    for w_ref, out_ref in ((wo_own, own_ref), (wo_other, other_ref)):
        grad = dot_cols(branch, w_ref[...]).astype(BF)
        for k in range(4):
            at = (-k) % 4 * 128
            out_ref[k] = grad[:, at : at + 128]


def branch_of(g_rows, terms, wo):
    return call(
        branch_body,
        (shaped((128, D), F32), shaped((128, D), BF)) + (shaped((4, 128, 128), BF),) * 2,
        in_specs=[in_vmem()] * 7,
        out_specs=(in_vmem(),) * 4,
        flops=2 * 128 * D * D,
        nbytes=4 * 2**20,
        name="branch",
    )(g_rows, *terms, *wo)


def columns_body(wq, wk, wv, wg, wu, gains_ref, out_ref):
    wq, wk, wv, wg, wu = (w[...].astype(F32) for w in (wq, wk, wv, wg, wu))
    gains = jnp.concatenate([gains_ref[...].astype(F32), jnp.zeros((8, 2 * FP), F32)], axis=1)
    gap = jnp.zeros((8, FP - FS), F32)
    for s in range(8):
        parts = [w[:, s * n : s * n + n] for w, n in ((wq, 128), (wk, HD), (wv, HD))]
        parts += [wg[:, s * FS : s * FS + FS], gap, wu[:, s * FS : s * FS + FS], gap]
        out_ref[s] = jnp.concatenate([jnp.concatenate(parts, axis=1), gains], axis=0).astype(BF)


def pack_columns(weights, gains):
    return call(
        columns_body,
        shaped((8, 16, 256 + 2 * FP), BF),
        in_specs=[in_vmem()] * 6,
        out_specs=in_vmem(),
        nbytes=2**20,
        name="pack_columns",
    )(*weights, gains)


def lines_body(cols_ref, downs_ref, out_ref):
    gains = cols_ref[0, :, :256].astype(F32)[8:]
    for s in range(1, 8):
        gains += cols_ref[s, :, :256].astype(F32)[8:]
    downs = downs_ref[...].astype(F32)
    outs, downs = downs[:8], jnp.concatenate([downs[8:], jnp.zeros((4, D), F32)], axis=0)
    parts = [cols_ref[s, :, :256].astype(F32)[:8] for s in range(8)] + [gains]
    parts += [outs[:, c : c + 256] for c in range(0, D, 256)]
    parts += [downs[:, c : c + 256] for c in range(0, D, 256)]
    line = jnp.concatenate(parts, axis=0).astype(BF)
    for k in range(16):
        out_ref[k] = line


def pack_lines(cols, downs):
    return call(
        lines_body,
        shaped((16, 264, 256), BF),
        in_specs=[in_vmem()] * 2,
        out_specs=in_vmem(),
        nbytes=3 * 2**20,
        name="pack_lines",
    )(cols, downs)


def units_body(cols_ref, out_ref):
    rows = [cols_ref[s, :, 256:].astype(F32)[:8] for s in range(8)]
    unit = jnp.concatenate(rows, axis=0).astype(BF)
    for k in range(16):
        out_ref[k] = unit


def pack_units(cols):
    return call(
        units_body,
        shaped((16, 64, 2 * FP), BF),
        in_specs=[in_vmem()],
        out_specs=in_vmem(),
        nbytes=3 * 2**20,
        name="pack_units",
    )(cols)


def sum_units_body(in_ref, cols_ref, down_ref):
    total = in_ref[0].astype(F32)
    for k in range(1, 16):
        total += in_ref[k].astype(F32)
    cols_ref[...] = total[:64]
    down_ref[...] = total[64:100, :D]


def sum_units(terms):
    return call(
        sum_units_body,
        (shaped((64, 2 * FP), F32), shaped((36, D), F32)),
        in_specs=[in_vmem()],
        out_specs=(in_vmem(),) * 2,
        nbytes=5 * 2**20,
        name="sum_units",
    )(terms)


def grads_body(lines_ref, units_ref, out_ref):
    heads = jnp.concatenate([lines_ref[64:72], jnp.zeros((8, 2 * FP), F32)], axis=1)
    for s in range(8):
        rows = slice(8 * s, 8 * s + 8)
        grads = jnp.concatenate([lines_ref[rows], units_ref[rows]], axis=1)
        out_ref[s] = jnp.concatenate([grads, heads], axis=0).astype(BF)


def pack_grads(lines, units):
    return call(
        grads_body,
        shaped((8, 16, 256 + 2 * FP), BF),
        in_specs=[in_vmem()] * 2,
        out_specs=in_vmem(),
        nbytes=2**20,
        name="pack_grads",
    )(lines, units)


def unpack_body(
    in_ref, wq, wk, wv, wg, wu, gain_attn, gain_ffn,
    gq_ref, gk_ref, gv_ref, gg_ref, gu_ref, attn_ref, ffn_ref, head_ref,
):
    blocks = [in_ref[s].astype(F32) for s in range(8)]

    def taken(w_ref, g_ref, at, n):
        grad = jnp.concatenate([b[:8, at : at + n] for b in blocks], axis=1)
        g_ref[...] = grad
        return jnp.sum(w_ref[...].astype(F32) * grad, axis=1, keepdims=True)

    attn = taken(wq, gq_ref, 0, 128) + taken(wk, gk_ref, 128, HD) + taken(wv, gv_ref, 192, HD)
    def across(column):
        lane = lax.broadcasted_iota(jnp.int32, (8, 8), 1)
        row = lax.broadcasted_iota(jnp.int32, (8, 8), 0)
        return jnp.sum(jnp.where(lane == row, column, 0.0), axis=0, keepdims=True)

    attn_ref[...] = across(attn) / gain_attn[...].astype(F32)
    feed = taken(wg, gg_ref, 256, FS) + taken(wu, gu_ref, 256 + FP, FS)
    ffn_ref[...] = across(feed) / gain_ffn[...].astype(F32)
    heads = blocks[0][8:, :256]
    for b in blocks[1:]:
        heads += b[8:, :256]
    head_ref[0:1] = heads[:1, :HD] + heads[:1, HD : 2 * HD]
    head_ref[1:2] = heads[:1, 2 * HD : 3 * HD]


def unpack_grads(cols, weights, gains):
    return call(
        unpack_body,
        tuple(shaped(w.shape, F32) for w in weights)
        + (shaped((1, 8), F32), shaped((1, 8), F32), shaped((2, HD), F32)),
        in_specs=[in_vmem()] * 8,
        out_specs=(in_vmem(),) * 8,
        nbytes=2**20,
        name="unpack_grads",
    )(cols, *weights, *gains)


def on_device(
    tokens, cotangent, block_of, attn_gain, ffn_gain, head_gains,
    w_query, w_key, w_value, w_out, w_gate, w_up, w_down,
):
    core, level = lax.axis_index("sp_1"), lax.axis_index("sp_0")
    cycle, half = lax.axis_index("cp_1"), lax.axis_index("cp_0")
    gains_f = head_gains.astype(F32)
    gq = jnp.tile(gains_f[0], 2)[None]
    gk = jnp.tile(gains_f[1], 2)[None]
    cosine, sine, table = row_tables(block_of, core, half, cycle, level)

    place = jnp.arange(8)[:, None] == lax.axis_index(SP)
    gains = jnp.stack([attn_gain, ffn_gain])[:, None, :]
    gains = jnp.where(place[None], gains, jnp.zeros((), BF)).reshape(1, 128)
    gains = jnp.pad(gains, ((0, 7), (0, 128)))
    columns = pack_columns((w_query, w_key, w_value, w_gate, w_up), gains)
    rows = own_first(jnp.stack([tokens, cotangent], axis=1), half)
    rows = jnp.stack([rows[0], pair(rows[1], "cp_0")], axis=1).reshape(2, 128, D)
    cols = exchange(after(columns, rows), SP)
    perm = [(d, (d % 16) * 8 + d // 16) for d in range(128)]
    downs = after(jnp.concatenate([w_out, w_down], axis=0), rows)
    downs = lax.ppermute(downs, DP_CP_SP, perm)
    line = pack_lines(cols, downs)
    lines = exchange(line, DC)
    gains = lines[:, 64, :128]
    gain_attn, gain_ffn = gains[:, :64].reshape(1, D), gains[:, 64:].reshape(1, D)

    both = around(after(rows, line).reshape(256, D), "sp_0")
    x_own = jnp.concatenate([a[:128] for a in both], axis=0)
    g_own = jnp.concatenate([a[128:] for a in both], axis=0)
    x_other = sibling(x_own)
    g_rows = rows[1]

    units = pack_units(after(cols, line))
    normed, raw, q, kv = project(
        x_own, x_other, gain_attn, lines, cosine, sine, gq, gk, (units,)
    )
    kvs = around(kv, "cp_1")
    units = exchange(after(units, *kvs[1:]), DC)
    g_other = sibling(after(g_own, q))
    wo_rows = jnp.concatenate([lines[:, r : r + 8] for r in range(72, 104, 8)], axis=2)
    wo_own = jnp.concatenate(around(after(wo_rows, *kvs[1:]).reshape(128, D), "sp_0"), axis=0)
    kvs = [a.reshape(2, 4, 2, 64, 128) for a in kvs]
    q = q.reshape(2, 4, 2, 64, 128)
    att, attT, lse = attend(table, q, kvs, ())
    att = att.reshape(ROWS, 128)
    wo = (wo_own, sibling(after(wo_own, att)))
    own = around(att, "sp_0")
    other = [sibling(a) for a in own]
    mixed_own, mixed_other, part_own, part_other, gw_units = ffn(
        own, other, (x_own, x_other), (g_own, g_other), gain_ffn, wo, units, lines
    )

    mids = sum_cores(part_own, part_other)
    terms = [ring(mids[k].astype(BF), "sp_0", 4 - k) for k in (1, 2, 3)]
    gw_units = exchange(gw_units, DC)
    mids = mids[:1] + terms
    grad_middle, branch, for_own, for_other = branch_of(g_rows, mids, wo)
    mixes = sum_cores(mixed_own, after(mixed_other, mids[0]))
    mixes = mixes[:1] + [a.astype(BF) for a in mixes[1:]]
    grad_att = jnp.stack([for_own, sibling(for_other)], axis=1)
    grad_att, *mixes = lax.optimization_barrier((grad_att, *mixes))
    grad_att = [grad_att[0]] + [ring(grad_att[k], "sp_0", k) for k in (1, 2, 3)]
    branch, *mixes = after((branch, *mixes), *grad_att)
    branches = around(branch, "sp_0")
    dq, *dkvs = attend_back(
        table, q, kvs, [a.reshape(2, 2, 64, 128) for a in grad_att], attT, lse
    )
    dkvs = [a.reshape(ROWS, 128) for a in after(tuple(dkvs), *branches[1:])]
    dkvs = dkvs[:1] + [ring(dkvs[k], "cp_1", 4 - k) for k in (1, 2, 3)]
    b_own = jnp.concatenate(after(branches, dq), axis=0)
    b_other = sibling(b_own)
    came = [ring(after(mixes[1], dq), "sp_0", 3)]
    came += [ring(after(mixes[k], *dkvs[1:]), "sp_0", 4 - k) for k in (2, 3)]
    gw_cols, gw_down = sum_units(gw_units)
    graw, line = heads_back(
        dq.reshape(ROWS, 128), dkvs, raw, cosine, sine, gq, gk, normed, att, b_own, b_other,
        (gw_cols,),
    )
    terms = jnp.sum(exchange(line, DC).astype(F32), axis=0)
    lasts = sum_cores(*rows_back(graw, x_own, x_other, gain_attn, lines, tuple(came)))
    lasts = [lasts[0]] + [a.astype(BF) for a in lasts[1:]]
    packed = pack_grads(terms, gw_cols)
    cols = exchange(packed, SP)
    last = grad_middle + lasts[0]
    mixed = mixes[0] + sum(a.astype(F32) for a in came)
    came = [ring(lasts[k], "sp_0", 4 - k) for k in (1, 2, 3)]
    last += sum(a.astype(F32) for a in after(came, packed))
    rows = jnp.stack([last, mixed]).astype(BF).reshape(2, 2, 64, D).swapaxes(0, 1)
    rows = own_first(jnp.stack([rows[0], pair(rows[1], "cp_0")]), half)
    grad_tokens, mixed = rows[:, 0], rows[:, 1]

    back = [(d, s) for s, d in perm]
    gw_out = jnp.concatenate([terms[r : r + 8] for r in range(72, 104, 8)], axis=1)
    downs = lax.ppermute(jnp.concatenate([gw_out, gw_down], axis=0), DP_CP_SP, back)
    downs = after(downs, rows)
    grad_w_out, grad_w_down = downs[:8], downs[8:]
    weights = (w_query, w_key, w_value, w_gate, w_up)
    gains = (attn_gain[None], ffn_gain[None])
    *grads, grad_attn_gain, grad_ffn_gain, heads = unpack_grads(cols, weights, gains)
    grad_w_query, grad_w_key, grad_w_value, grad_w_gate, grad_w_up = grads
    return (
        mixed,
        grad_tokens,
        grad_attn_gain[0],
        grad_ffn_gain[0],
        heads,
        grad_w_query,
        grad_w_key,
        grad_w_value,
        grad_w_out,
        grad_w_gate,
        grad_w_up,
        grad_w_down,
    )


def solution(mesh):
    torus = Mesh(
        mesh.devices.reshape(mesh.shape["dp"], 2, 4, 4, 2), ("dp", "cp_0", "cp_1", "sp_0", "sp_1")
    )
    rows, split = P("dp", CP_SP, None), P(DP_CP_SP, None)
    in_specs = (rows, rows, P(), P(DP_CP_SP), P(DP_CP_SP), P()) + (split,) * 7
    out_specs = (rows, rows, P(DP_CP_SP), P(DP_CP_SP), P()) + (split,) * 7
    return jax.shard_map(
        on_device, mesh=torus, in_specs=in_specs, out_specs=out_specs, check_vma=False
    )
```

```python
from functools import partial

import jax
import jax.numpy as jnp
from jax import lax
from jax.experimental import pallas as pl
from jax.experimental.pallas import tpu as pltpu
from jax.sharding import Mesh
from jax.sharding import PartitionSpec as P

SP = ("sp_0", "sp_1")
DC = ("dp", "cp_0", "cp_1")
DP_CP_SP = ("dp", "cp_0", "cp_1", "sp_0", "sp_1")
CP_SP = ("cp_0", "cp_1", "sp_0", "sp_1")

EPSILON = 1e-05
ROPE_BASE = 1000000.0
BF = jnp.bfloat16
F32 = jnp.float32

D = 1024
HD = 64
FF = 4608
FS = FF // 8
FP = 640
BLK = 256
ROWS = 1024
TILE = 256
VMEM_LIMIT = 56 * 1024 * 1024


def dot(left, right):
    return jnp.dot(left, right, preferred_element_type=F32)


def dot_rows(left, right):
    return lax.dot_general(left, right, (((0,), (0,)), ((), ())), preferred_element_type=F32)


def dot_cols(left, right):
    return lax.dot_general(left, right, (((1,), (1,)), ((), ())), preferred_element_type=F32)


def call(body, out, **kw):
    flops = kw.pop("flops", 0)
    nbytes = kw.pop("nbytes", 0)
    after = kw.pop("after", ())
    if after:
        inner, count = body, len(after)
        kw["in_specs"] = [pl.BlockSpec(memory_space=pl.ANY)] * count + list(kw["in_specs"])

        def body(*refs):
            return inner(*refs[count:])

        return partial(call(body, out, flops=flops, nbytes=nbytes, **kw), *after)
    return pl.pallas_call(
        body,
        out_shape=out,
        compiler_params=pltpu.CompilerParams(vmem_limit_bytes=VMEM_LIMIT),
        cost_estimate=pl.CostEstimate(flops=flops, bytes_accessed=nbytes, transcendentals=0),
        **kw,
    )


def shaped(shape, dtype):
    return jax.ShapeDtypeStruct(shape, dtype)


def ring(x, axis, k):
    return lax.ppermute(x, axis, [(i, (i + k) % 4) for i in range(4)])


def pair(x, axis):
    return lax.ppermute(x, axis, [(0, 1), (1, 0)])


def sibling(x):
    return pair(x, "sp_1")


def exchange(x, axis):
    return lax.all_to_all(x, axis, 0, 0, tiled=True)


def after(x, *first):
    return lax.optimization_barrier((x, *first))[0]


def around(x, axis):
    return [x] + [ring(x, axis, k) for k in (1, 2, 3)]


def own_first(both, half):
    return jnp.where(half == 0, both, both[::-1])


def swapped(rows):
    return jnp.concatenate([rows[0], pair(rows[1], "cp_0")], axis=0)


def sum_cores(own, other):
    came = sibling(other)
    return [
        own[r : r + 128].astype(F32) + came[r : r + 128].astype(F32) for r in range(0, 512, 128)
    ]


def rms_of(x):
    return lax.rsqrt(jnp.mean(x * x, axis=-1, keepdims=True) + EPSILON)


def norm_back(x, gain, upstream):
    r = rms_of(x)
    n = x * r
    scaled = upstream * gain
    return r * (scaled - n * jnp.mean(scaled * n, axis=-1, keepdims=True))


def low_half(shape):
    return lax.broadcasted_iota(jnp.int32, shape, 1) < HD


def head_mean(v):
    low = low_half(v.shape)
    first = jnp.sum(jnp.where(low, v, 0.0), axis=1, keepdims=True)
    second = jnp.sum(jnp.where(low, 0.0, v), axis=1, keepdims=True)
    return jnp.where(low, first, second) * (1.0 / HD)


def swap_halves(v):
    lane = lax.broadcasted_iota(jnp.int32, v.shape, 1)
    return jnp.where(lane % HD < HD // 2, pltpu.roll(v, 96, 1), pltpu.roll(v, 32, 1))


def row_tables(block_of, core, half, cycle, level):
    slots = jnp.arange(16, dtype=jnp.int32)
    blocks = block_of.reshape(2, 4, 2)
    blocks = jnp.where(half == 0, blocks, blocks[::-1])
    local = lax.dynamic_index_in_dim(blocks, cycle, 1, keepdims=False)
    z = (level - jnp.arange(4, dtype=jnp.int32)) % 4
    pick = (z // 2)[None, :] == 1
    by_z = jnp.where(pick, local[:, 1:], local[:, :1]).T
    entries = HD // 2
    inverse = ROPE_BASE ** (-(2.0 * jnp.arange(entries, dtype=F32)) / HD)
    inverse = jnp.tile(inverse, 4)
    sign = jnp.tile(jnp.concatenate([-jnp.ones(entries, F32), jnp.ones(entries, F32)]), 2)
    first = (by_z.reshape(8) * BLK).astype(F32)[:, None] * inverse[None]
    rel = jnp.arange(2, dtype=jnp.int32)[:, None, None]
    row = jnp.arange(64, dtype=jnp.int32)[None, None, :]
    inner = ((z % 2)[None, :, None] * 128 + (rel ^ core) * 64 + row).reshape(512)
    inner = inner.astype(F32)[:, None] * inverse[None]
    ca, sa = (f(first).reshape(1, 4, 2, 1, 128) for f in (jnp.cos, jnp.sin))
    cb, sb = (f(inner).reshape(2, 4, 1, 64, 128) for f in (jnp.cos, jnp.sin))
    cosine = (ca * cb - sa * sb).reshape(ROWS, 128)
    sine = ((sa * cb + ca * sb) * sign).reshape(ROWS, 128)
    distance = (cycle - (slots >> 1)) & 3
    at = distance * 4 + ((slots >> 3) ^ half) * 2 + (slots & 1)
    slot_at = jnp.sum(jnp.where(block_of[None, :] == slots[:, None], at[None, :], 0), axis=1)
    place = (level - jnp.arange(4, dtype=jnp.int32)) & 3
    table = jnp.concatenate([local.reshape(4), place, slot_at, core[None]]).astype(jnp.int32)
    return cosine, sine, table


def project_body(own_ref, other_ref, gain_ref, w_ref, cos_ref, sin_ref, gq_ref, gk_ref, n_ref, raw_ref, q_ref, kv_ref):
    x = picked(own_ref, other_ref).astype(F32)
    normed = (x * rms_of(x) * gain_ref[...].astype(F32)).astype(BF)
    n_ref[...] = normed
    raw = dot(normed, w_ref[:, :64].reshape(D, 256))
    raw_ref[...] = raw
    cosine, sine = cos_ref[...], sin_ref[...]

    def turned(v, gain):
        v = v * lax.rsqrt(head_mean(v * v) + EPSILON) * gain
        return (v * cosine + swap_halves(v) * sine).astype(BF)

    q_ref[...] = turned(raw[:, :128], gq_ref[...]) * jnp.asarray(0.125, BF)
    right = raw[:, 128:]
    kv_ref[...] = jnp.where(low_half(right.shape), turned(right, gk_ref[...]), right.astype(BF))


def picked(own_ref, other_ref):
    return jnp.where(pl.program_id(0) < 2, own_ref[...], other_ref[...])


def halves(width):
    return [
        pl.BlockSpec((TILE, width), lambda t: (jnp.minimum(t, 1), 0)),
        pl.BlockSpec((TILE, width), lambda t: (jnp.maximum(t - 2, 0), 0)),
    ]


def tiles(width):
    return pl.BlockSpec((TILE, width), lambda t: (t, 0))


def whole(*shape):
    return pl.BlockSpec(shape, lambda t: (0,) * len(shape))


def project(x, other, gain, w, cosine, sine, gq, gk, after):
    return call(
        project_body,
        (
            shaped((ROWS, D), BF),
            shaped((ROWS, 256), F32),
            shaped((ROWS, 128), BF),
            shaped((ROWS, 128), BF),
        ),
        grid=(ROWS // TILE,),
        in_specs=halves(D) + [whole(1, D), whole(16, 264, 256), tiles(128), tiles(128), whole(1, 128), whole(1, 128)],
        out_specs=(tiles(D), tiles(256), tiles(128), tiles(128)),
        flops=2 * ROWS * D * 256,
        nbytes=7 * 2**20,
        after=after,
        name="project",
    )(x, other, gain, w, cosine, sine, gq, gk)


def heads_back_body(
    dq_ref, k0_ref, k1_ref, k2_ref, k3_ref, raw_ref, cos_ref, sin_ref, gq_ref, gk_ref, n_ref,
    att_ref, own_ref, other_ref, graw_ref, line_ref, gw_acc, out_acc, head_acc,
):
    step = pl.program_id(0)

    @pl.when(step == 0)
    def _():
        gw_acc[...] = jnp.zeros_like(gw_acc)
        out_acc[...] = jnp.zeros_like(out_acc)
        head_acc[...] = jnp.zeros_like(head_acc)

    cosine, sine = cos_ref[...], sin_ref[...]

    def back(raw, grad, gain):
        r = lax.rsqrt(head_mean(raw * raw) + EPSILON)
        n = raw * r
        up = grad * cosine + swap_halves(grad * sine)
        scaled = up * gain
        return r * (scaled - n * head_mean(scaled * n)), jnp.sum(up * n, axis=0, keepdims=True)

    raw = raw_ref[...]
    graw_q, gain_q = back(raw[:, :128], dq_ref[...], gq_ref[...])
    dkv = (k0_ref[...].astype(F32) + k1_ref[...].astype(F32)) + (
        k2_ref[...].astype(F32) + k3_ref[...].astype(F32)
    )
    graw_k, gain_k = back(raw[:, 128:], dkv, gk_ref[...])
    gain_k = jnp.where(low_half(gain_k.shape), gain_k, 0.0)
    head_acc[...] += jnp.concatenate([gain_q, gain_k], axis=1)
    graw = jnp.concatenate([graw_q, jnp.where(low_half(dkv.shape), graw_k, dkv)], axis=1).astype(BF)
    graw_ref[...] = graw
    gw_acc[...] += dot_rows(n_ref[...], graw)
    out_acc[...] += dot_rows(att_ref[...], picked(own_ref, other_ref))

    @pl.when(step == pl.num_programs(0) - 1)
    def _():
        heads = jnp.broadcast_to(head_acc[...], (8, 256))
        for k in range(16):
            rows = out_acc[8 * k : 8 * k + 8]
            parts = [gw_acc[64 * k : 64 * k + 64], heads]
            parts += [rows[:, c : c + 256] for c in range(0, D, 256)]
            line_ref[k] = jnp.concatenate(parts, axis=0).astype(BF)


def heads_back(dq, dkvs, raw, cosine, sine, gq, gk, normed, att, b_own, b_other, after):
    return call(
        heads_back_body,
        (shaped((ROWS, 256), BF), shaped((16, 104, 256), BF)),
        grid=(ROWS // TILE,),
        in_specs=[tiles(128)] * 5
        + [tiles(256), tiles(128), tiles(128), whole(1, 128), whole(1, 128), tiles(D), tiles(128)]
        + halves(D),
        out_specs=(tiles(256), whole(16, 104, 256)),
        scratch_shapes=[
            pltpu.VMEM((D, 256), F32),
            pltpu.VMEM((128, D), F32),
            pltpu.VMEM((1, 256), F32),
        ],
        flops=2 * ROWS * D * 384,
        nbytes=10 * 2**20,
        after=after,
        name="heads_back",
    )(dq, *dkvs, raw, cosine, sine, gq, gk, normed, att, b_own, b_other)


def rows_back_body(graw_ref, own_ref, other_ref, gain_ref, w_ref, out_own, out_other):
    x = picked(own_ref, other_ref).astype(F32)
    grad = dot_cols(graw_ref[...], w_ref[:, :64].reshape(D, 256))
    part = norm_back(x, gain_ref[...].astype(F32), grad).astype(BF)

    @pl.when(pl.program_id(0) < 2)
    def _():
        out_own[...] = part

    @pl.when(pl.program_id(0) >= 2)
    def _():
        out_other[...] = part


def rows_back(graw, x, other, gain, w, after):
    return call(
        rows_back_body,
        (shaped((ROWS // 2, D), BF),) * 2,
        grid=(ROWS // TILE,),
        in_specs=[tiles(256)] + halves(D) + [whole(1, D), whole(16, 264, 256)],
        out_specs=tuple(halves(D)),
        flops=2 * ROWS * D * 256,
        nbytes=5 * 2**20,
        after=after,
        name="rows_back",
    )(graw, x, other, gain, w)


def stored(tab_ref, ref, half, h):
    return jnp.concatenate(
        [ref[c, tab_ref[4 + 2 * h + zz], half] for c in range(2) for zz in range(2)], axis=0
    )


def store(tab_ref, ref, half, h, block):
    for c in range(2):
        for zz in range(2):
            row = (c * 2 + zz) * 64
            ref[c, tab_ref[4 + 2 * h + zz], half] = block[row : row + 64]


def heads_across(block):
    flat = block.astype(F32).T
    return jnp.concatenate([flat[:HD], flat[HD:]], axis=1)


def diagonal_mask(core):
    def place(t):
        return ((t >> 6) & 1) * 128 + ((t >> 7) ^ core) * 64 + (t & 63)

    keys = place(lax.broadcasted_iota(jnp.int32, (BLK, 2 * BLK), 0))
    queries = place(lax.broadcasted_iota(jnp.int32, (BLK, 2 * BLK), 1) & 255)
    return keys <= queries


def pair_at(tab_ref, i, o):
    count = tab_ref[2 * o]
    first = i < count
    qb = 2 * o + jnp.where(first, 0, 1)
    slot = tab_ref[8 + jnp.where(first, i, i - count)]
    return qb, slot


def attend_body(tab_ref, q_ref, kv0, kv1, kv2, kv3, att_ref, attT_ref, lse_ref, qT, kv, vT, acc):
    zeros = jnp.zeros((HD, 2 * BLK), BF)
    for qb in range(4):
        qT[qb, :HD] = heads_across(stored(tab_ref, q_ref, qb // 2, qb % 2)).astype(BF)
        qT[qb, HD:] = zeros
    for slot in range(16):
        block = stored(tab_ref, (kv0, kv1, kv2, kv3)[slot // 4], (slot >> 1) & 1, slot & 1)
        kv[slot] = block
        flat = block.astype(F32).T
        vT[slot] = jnp.concatenate([jnp.ones((16, BLK), F32), flat[HD:]], axis=0).astype(BF)
    acc[...] = jnp.zeros_like(acc)

    def pair(qb, slot, mask=None):
        p = jnp.exp(dot(kv[slot], qT[qb]))
        if mask is not None:
            p = jnp.where(mask, p, 0.0)
        acc[qb] += dot(vT[slot], p.astype(BF))

    def step(i, carry):
        for o in range(2):
            pair(*pair_at(tab_ref, i, o))
        return carry

    lax.fori_loop(0, 15, step, 0, unroll=15)
    mask = diagonal_mask(tab_ref[24])
    for qb in range(4):
        pair(qb, tab_ref[8 + tab_ref[qb]], mask)
        total = acc[qb, :1]
        out = acc[qb, 16:] / total
        flat = jnp.concatenate([out[:, :BLK], out[:, BLK:]], axis=0)
        attT_ref[qb] = flat
        lse_ref[qb] = jnp.log(total)
        store(tab_ref, att_ref, qb // 2, qb % 2, flat.T.astype(BF))


def in_smem():
    return pl.BlockSpec(memory_space=pltpu.SMEM)


def in_vmem():
    return pl.BlockSpec(memory_space=pltpu.VMEM)


def attend(table, q, kvs, after):
    return call(
        attend_body,
        (
            shaped((2, 4, 2, 64, 128), BF),
            shaped((4, 128, BLK), F32),
            shaped((4, 1, 2 * BLK), F32),
        ),
        in_specs=[in_smem()] + [in_vmem()] * 5,
        out_specs=(in_vmem(), in_vmem(), in_vmem()),
        scratch_shapes=[
            pltpu.VMEM((4, 128, 2 * BLK), BF),
            pltpu.VMEM((16, BLK, 128), BF),
            pltpu.VMEM((16, HD + 16, BLK), BF),
            pltpu.VMEM((4, HD + 16, 2 * BLK), F32),
        ],
        flops=34 * 4 * BLK * 2 * BLK * 128,
        nbytes=2 * 2**20,
        after=after,
        name="attend",
    )(table, q, *kvs)


def attend_back_body(
    tab_ref, q_ref, kv0, kv1, kv2, kv3, g0, g1, g2, g3, attT_ref, lse_ref,
    dq_ref, dkv0, dkv1, dkv2, dkv3, g_ref, qT, gT, qn, gn, kv, kT, delta, dqT, dkv,
):
    for k, ref in enumerate((g0, g1, g2, g3)):
        g_ref[0, k], g_ref[1, k] = ref[0], ref[1]
    zeros = jnp.zeros((HD, 2 * BLK), F32)
    for qb in range(4):
        across = jnp.concatenate([heads_across(stored(tab_ref, q_ref, qb // 2, qb % 2)), zeros], axis=0)
        qT[qb] = across.astype(BF)
        qn[qb] = across.T.astype(BF)
        g_across = heads_across(stored(tab_ref, g_ref, qb // 2, qb % 2))
        out = attT_ref[qb]
        out = jnp.concatenate([out[:HD], out[HD:]], axis=1)
        delta[qb] = jnp.sum(g_across * out, axis=0, keepdims=True)
        g_across = jnp.concatenate([zeros, g_across], axis=0)
        gT[qb] = g_across.astype(BF)
        gn[qb] = g_across.T.astype(BF)
    for slot in range(16):
        block = stored(tab_ref, (kv0, kv1, kv2, kv3)[slot // 4], (slot >> 1) & 1, slot & 1)
        kv[slot] = block
        kT[slot] = block.astype(F32).T[:HD].astype(BF)
    dqT[...] = jnp.zeros_like(dqT)
    dkv[...] = jnp.zeros_like(dkv)

    def pair(qb, slot, mask=None):
        keys = kv[slot]
        p = jnp.exp(dot(keys, qT[qb]) - lse_ref[qb])
        if mask is not None:
            p = jnp.where(mask, p, 0.0)
        ds = (p * (dot(keys, gT[qb]) - delta[qb])).astype(BF)
        dkv[slot] += dot(ds, qn[qb]) + dot(p.astype(BF), gn[qb])
        dqT[qb] += dot(kT[slot], ds)

    def step(i, carry):
        for o in range(2):
            pair(*pair_at(tab_ref, i, o))
        return carry

    lax.fori_loop(0, 15, step, 0, unroll=15)
    mask = diagonal_mask(tab_ref[24])
    for qb in range(4):
        pair(qb, tab_ref[8 + tab_ref[qb]], mask)
        flat = jnp.concatenate([dqT[qb, :, :BLK], dqT[qb, :, BLK:]], axis=0)
        store(tab_ref, dq_ref, qb // 2, qb % 2, flat.T * 0.125)
    for slot in range(16):
        out = (dkv0, dkv1, dkv2, dkv3)[slot // 4]
        store(tab_ref, out, (slot >> 1) & 1, slot & 1, dkv[slot].astype(BF))


def attend_back(table, q, kvs, gs, attT, lse):
    return call(
        attend_back_body,
        (shaped((2, 4, 2, 64, 128), F32),) + (shaped((2, 4, 2, 64, 128), BF),) * 4,
        in_specs=[in_smem()] + [in_vmem()] * 11,
        out_specs=(in_vmem(),) * 5,
        scratch_shapes=[
            pltpu.VMEM((2, 4, 2, 64, 128), BF),
            pltpu.VMEM((4, 128, 2 * BLK), BF),
            pltpu.VMEM((4, 128, 2 * BLK), BF),
            pltpu.VMEM((4, 2 * BLK, 128), BF),
            pltpu.VMEM((4, 2 * BLK, 128), BF),
            pltpu.VMEM((16, BLK, 128), BF),
            pltpu.VMEM((16, HD, BLK), BF),
            pltpu.VMEM((4, 1, 2 * BLK), F32),
            pltpu.VMEM((4, HD, 2 * BLK), F32),
            pltpu.VMEM((16, BLK, 128), F32),
        ],
        flops=34 * 10 * BLK * 2 * BLK * 128,
        nbytes=4 * 2**20,
        name="attend_back",
    )(table, q, *kvs, *gs, attT, lse)


def ffn_body(
    a0, a1, a2, a3, b0, b1, b2, b3, x_own, x_other, g_own, g_other, gain_ref,
    wo_own, wo_other, units_ref, lines_ref,
    mixed_own, mixed_other, part_own, part_other, gw_ref, wd, n_all, p_all, h_all,
):
    step = pl.program_id(0)

    @pl.when(step == 0)
    def _():
        rows = []
        for k in range(16):
            parts = [lines_ref[k, r : r + 40].astype(F32)[:36] for r in range(104, 264, 40)]
            rows.append(jnp.concatenate(parts, axis=1))
        rows.append(jnp.zeros((FP - FS, D), F32))
        wd[...] = jnp.concatenate(rows, axis=0).astype(BF)

    core, first = step // 2, step % 2 * 2
    middle = picked(x_own, x_other).astype(F32)
    for c, (refs, w_ref) in enumerate((((a0, a1, a2, a3), wo_own), ((b0, b1, b2, b3), wo_other))):
        pieces = []
        for k, ref in enumerate(refs):
            at = [(core ^ c) * 512 + ((first + j - k) & 3) * 128 for j in range(2)]
            pieces.append(jnp.concatenate([ref[pl.ds(r, 128)] for r in at], axis=0))
        middle += dot(jnp.concatenate(pieces, axis=1), w_ref[...])
    gain = gain_ref[...].astype(F32)
    normed = (middle * rms_of(middle) * gain).astype(BF)
    wgu = units_ref[...].reshape(D, 2 * FP)
    pre = dot(normed, wgu)
    gate, up = pre[:, :FP], pre[:, FP:]
    s = 1.0 / (1.0 + jnp.exp(-gate))
    act = gate * s
    hidden = (act * up).astype(BF)
    row = lax.broadcasted_iota(jnp.int32, (TILE, 1), 0)
    here = jnp.logical_and(step == 0, row < 128)
    mixed = (dot(hidden, wd[...]) + jnp.where(here, middle, 0.0)).astype(BF)
    r = pl.ds(pl.multiple_of(step % 2 * TILE, TILE), TILE)
    g = jnp.where(step < 2, g_own[r], g_other[r])
    gh = dot_cols(g, wd[...])
    at = pl.ds(pl.multiple_of(step * TILE, TILE), TILE)
    h_all[at], n_all[at] = hidden, normed
    gpre = jnp.concatenate([gh * up * s * (1.0 + gate * (1.0 - s)), gh * act], axis=1).astype(BF)
    p_all[at] = gpre
    part = norm_back(middle, gain, dot_cols(gpre, wgu)).astype(BF)

    @pl.when(step < 2)
    def _():
        mixed_own[...] = mixed
        part_own[...] = part

    @pl.when(step >= 2)
    def _():
        mixed_other[...] = mixed
        part_other[...] = part

    @pl.when(step == pl.num_programs(0) - 1)
    def _():
        for k in range(4):
            cols = dot_rows(n_all[:, 256 * k : 256 * k + 256], p_all[...])
            for j in range(4):
                gw_ref[4 * k + j, :64] = cols[64 * j : 64 * j + 64].astype(BF)
        h = h_all[...]
        downs = dot_rows(h[:512], g_own[...]) + dot_rows(h[512:], g_other[...])
        for k in range(16):
            rows = jnp.concatenate([downs[36 * k : 36 * k + 36], jnp.zeros((4, D), F32)], axis=0)
            rows = jnp.concatenate([rows, jnp.zeros((40, 2 * FP - D), F32)], axis=1)
            gw_ref[k, 64:] = rows.astype(BF)


def ffn(own, other, x, g, gain, wo, units, lines):
    return call(
        ffn_body,
        (shaped((ROWS // 2, D), BF),) * 4 + (shaped((16, 104, 2 * FP), BF),),
        grid=(ROWS // TILE,),
        in_specs=[whole(ROWS, 128)] * 8
        + halves(D)
        + [whole(ROWS // 2, D)] * 2
        + [whole(1, D), whole(D // 2, D), whole(D // 2, D)]
        + [whole(16, 64, 2 * FP), whole(16, 264, 256)],
        out_specs=tuple(halves(D) * 2) + (whole(16, 104, 2 * FP),),
        scratch_shapes=[
            pltpu.VMEM((FP, D), BF),
            pltpu.VMEM((ROWS, D), BF),
            pltpu.VMEM((ROWS, 2 * FP), BF),
            pltpu.VMEM((ROWS, FP), BF),
        ],
        flops=2 * ROWS * D * (D + 9 * FP),
        nbytes=24 * 2**20,
        name="ffn",
    )(*own, *other, *x, *g, gain, *wo, units, lines)


def branch_body(g_ref, t0, t1, t2, t3, wo_own, wo_other, mid_ref, branch_ref, own_ref, other_ref):
    total = g_ref[...].astype(F32) + t0[...] + t1[...].astype(F32)
    total += t2[...].astype(F32) + t3[...].astype(F32)
    mid_ref[...] = total
    branch = total.astype(BF)
    branch_ref[...] = branch
    for w_ref, out_ref in ((wo_own, own_ref), (wo_other, other_ref)):
        grad = dot_cols(branch, w_ref[...]).astype(BF)
        for k in range(4):
            at = (-k) % 4 * 128
            out_ref[k] = grad[:, at : at + 128]


def branch_of(g_rows, terms, wo):
    return call(
        branch_body,
        (shaped((128, D), F32), shaped((128, D), BF)) + (shaped((4, 128, 128), BF),) * 2,
        in_specs=[in_vmem()] * 7,
        out_specs=(in_vmem(),) * 4,
        flops=2 * 128 * D * D,
        nbytes=4 * 2**20,
        name="branch",
    )(g_rows, *terms, *wo)


def columns_body(wq, wk, wv, wg, wu, gains_ref, out_ref):
    wq, wk, wv, wg, wu = (w[...].astype(F32) for w in (wq, wk, wv, wg, wu))
    gains = jnp.concatenate([gains_ref[...].astype(F32), jnp.zeros((8, 2 * FP), F32)], axis=1)
    gap = jnp.zeros((8, FP - FS), F32)
    for s in range(8):
        parts = [w[:, s * n : s * n + n] for w, n in ((wq, 128), (wk, HD), (wv, HD))]
        parts += [wg[:, s * FS : s * FS + FS], gap, wu[:, s * FS : s * FS + FS], gap]
        out_ref[s] = jnp.concatenate([jnp.concatenate(parts, axis=1), gains], axis=0).astype(BF)


def pack_columns(weights, gains):
    return call(
        columns_body,
        shaped((8, 16, 256 + 2 * FP), BF),
        in_specs=[in_vmem()] * 6,
        out_specs=in_vmem(),
        nbytes=2**20,
        name="pack_columns",
    )(*weights, gains)


def lines_body(cols_ref, downs_ref, out_ref):
    gains = cols_ref[0, :, :256].astype(F32)[8:]
    for s in range(1, 8):
        gains += cols_ref[s, :, :256].astype(F32)[8:]
    downs = downs_ref[...].astype(F32)
    outs, downs = downs[:8], jnp.concatenate([downs[8:], jnp.zeros((4, D), F32)], axis=0)
    parts = [cols_ref[s, :, :256].astype(F32)[:8] for s in range(8)] + [gains]
    parts += [outs[:, c : c + 256] for c in range(0, D, 256)]
    parts += [downs[:, c : c + 256] for c in range(0, D, 256)]
    line = jnp.concatenate(parts, axis=0).astype(BF)
    for k in range(16):
        out_ref[k] = line


def pack_lines(cols, downs, after):
    return call(
        lines_body,
        shaped((16, 264, 256), BF),
        in_specs=[in_vmem()] * 2,
        out_specs=in_vmem(),
        nbytes=3 * 2**20,
        after=after,
        name="pack_lines",
    )(cols, downs)


def units_body(cols_ref, out_ref):
    rows = [cols_ref[s, :, 256:].astype(F32)[:8] for s in range(8)]
    unit = jnp.concatenate(rows, axis=0).astype(BF)
    for k in range(16):
        out_ref[k] = unit


def pack_units(cols):
    return call(
        units_body,
        shaped((16, 64, 2 * FP), BF),
        in_specs=[in_vmem()],
        out_specs=in_vmem(),
        nbytes=3 * 2**20,
        name="pack_units",
    )(cols)


def sum_units_body(in_ref, cols_ref, down_ref):
    total = in_ref[0].astype(F32)
    for k in range(1, 16):
        total += in_ref[k].astype(F32)
    cols_ref[...] = total[:64]
    down_ref[...] = total[64:100, :D]


def sum_units(terms):
    return call(
        sum_units_body,
        (shaped((64, 2 * FP), F32), shaped((36, D), F32)),
        in_specs=[in_vmem()],
        out_specs=(in_vmem(),) * 2,
        nbytes=5 * 2**20,
        name="sum_units",
    )(terms)


def grads_body(lines_ref, units_ref, out_ref):
    heads = jnp.concatenate([lines_ref[64:72], jnp.zeros((8, 2 * FP), F32)], axis=1)
    for s in range(8):
        rows = slice(8 * s, 8 * s + 8)
        grads = jnp.concatenate([lines_ref[rows], units_ref[rows]], axis=1)
        out_ref[s] = jnp.concatenate([grads, heads], axis=0).astype(BF)


def pack_grads(lines, units):
    return call(
        grads_body,
        shaped((8, 16, 256 + 2 * FP), BF),
        in_specs=[in_vmem()] * 2,
        out_specs=in_vmem(),
        nbytes=2**20,
        name="pack_grads",
    )(lines, units)


def unpack_body(
    in_ref, wq, wk, wv, wg, wu, gain_attn, gain_ffn,
    gq_ref, gk_ref, gv_ref, gg_ref, gu_ref, attn_ref, ffn_ref, head_ref,
):
    blocks = [in_ref[s].astype(F32) for s in range(8)]

    def taken(w_ref, g_ref, at, n):
        grad = jnp.concatenate([b[:8, at : at + n] for b in blocks], axis=1)
        g_ref[...] = grad
        return jnp.sum(w_ref[...].astype(F32) * grad, axis=1, keepdims=True)

    attn = taken(wq, gq_ref, 0, 128) + taken(wk, gk_ref, 128, HD) + taken(wv, gv_ref, 192, HD)
    def across(column):
        lane = lax.broadcasted_iota(jnp.int32, (8, 8), 1)
        row = lax.broadcasted_iota(jnp.int32, (8, 8), 0)
        return jnp.sum(jnp.where(lane == row, column, 0.0), axis=0, keepdims=True)

    attn_ref[...] = across(attn) / gain_attn[...].astype(F32)
    feed = taken(wg, gg_ref, 256, FS) + taken(wu, gu_ref, 256 + FP, FS)
    ffn_ref[...] = across(feed) / gain_ffn[...].astype(F32)
    heads = blocks[0][8:, :256]
    for b in blocks[1:]:
        heads += b[8:, :256]
    head_ref[0:1] = heads[:1, :HD] + heads[:1, HD : 2 * HD]
    head_ref[1:2] = heads[:1, 2 * HD : 3 * HD]


def unpack_grads(cols, weights, gains):
    return call(
        unpack_body,
        tuple(shaped(w.shape, F32) for w in weights)
        + (shaped((1, 8), F32), shaped((1, 8), F32), shaped((2, HD), F32)),
        in_specs=[in_vmem()] * 8,
        out_specs=(in_vmem(),) * 8,
        nbytes=2**20,
        name="unpack_grads",
    )(cols, *weights, *gains)


def on_device(
    tokens, cotangent, block_of, attn_gain, ffn_gain, head_gains,
    w_query, w_key, w_value, w_out, w_gate, w_up, w_down,
):
    core, level = lax.axis_index("sp_1"), lax.axis_index("sp_0")
    cycle, half = lax.axis_index("cp_1"), lax.axis_index("cp_0")
    gains_f = head_gains.astype(F32)
    gq = jnp.tile(gains_f[0], 2)[None]
    gk = jnp.tile(gains_f[1], 2)[None]
    cosine, sine, table = row_tables(block_of, core, half, cycle, level)

    place = jnp.arange(8)[:, None] == lax.axis_index(SP)
    gains = jnp.stack([attn_gain, ffn_gain])[:, None, :]
    gains = jnp.where(place[None], gains, jnp.zeros((), BF)).reshape(1, 128)
    gains = jnp.pad(gains, ((0, 7), (0, 128)))
    rows = own_first(jnp.stack([tokens, cotangent], axis=1), half)
    rows = jnp.stack([rows[0], pair(rows[1], "cp_0")], axis=1).reshape(2, 128, D)
    columns = pack_columns((w_query, w_key, w_value, w_gate, w_up), gains)
    cols = exchange(columns, SP)
    perm = [(d, (d % 16) * 8 + d // 16) for d in range(128)]
    downs = lax.ppermute(jnp.concatenate([w_out, w_down], axis=0), DP_CP_SP, perm)
    line = pack_lines(cols, downs, (rows,))
    lines = exchange(line, DC)
    gains = lines[:, 64, :128]
    gain_attn, gain_ffn = gains[:, :64].reshape(1, D), gains[:, 64:].reshape(1, D)

    both = around(after(rows, line).reshape(256, D), "sp_0")
    x_own = jnp.concatenate([a[:128] for a in both], axis=0)
    g_own = jnp.concatenate([a[128:] for a in both], axis=0)
    x_other = sibling(x_own)
    g_rows = rows[1]

    units = pack_units(after(cols, line))
    normed, raw, q, kv = project(
        x_own, x_other, gain_attn, lines, cosine, sine, gq, gk, (units,)
    )
    kvs = around(kv, "cp_1")
    units = exchange(after(units, *kvs[1:]), DC)
    g_other = sibling(after(g_own, q))
    wo_rows = jnp.concatenate([lines[:, r : r + 8] for r in range(72, 104, 8)], axis=2)
    wo_own = jnp.concatenate(around(after(wo_rows, *kvs[1:]).reshape(128, D), "sp_0"), axis=0)
    kvs = [a.reshape(2, 4, 2, 64, 128) for a in kvs]
    q = q.reshape(2, 4, 2, 64, 128)
    att, attT, lse = attend(table, q, kvs, ())
    att = att.reshape(ROWS, 128)
    wo = (wo_own, sibling(after(wo_own, att)))
    own = around(att, "sp_0")
    other = [sibling(a) for a in own]
    mixed_own, mixed_other, part_own, part_other, gw_units = ffn(
        own, other, (x_own, x_other), (g_own, g_other), gain_ffn, wo, units, lines
    )

    mids = sum_cores(part_own, part_other)
    terms = [ring(mids[k].astype(BF), "sp_0", 4 - k) for k in (1, 2, 3)]
    gw_units = exchange(gw_units, DC)
    mids = mids[:1] + terms
    grad_middle, branch, for_own, for_other = branch_of(g_rows, mids, wo)
    mixes = sum_cores(mixed_own, after(mixed_other, mids[0]))
    mixes = mixes[:1] + [a.astype(BF) for a in mixes[1:]]
    grad_att = jnp.stack([for_own, sibling(for_other)], axis=1)
    grad_att, *mixes = lax.optimization_barrier((grad_att, *mixes))
    grad_att = [grad_att[0]] + [ring(grad_att[k], "sp_0", k) for k in (1, 2, 3)]
    branch, *mixes = after((branch, *mixes), *grad_att)
    branches = around(branch, "sp_0")
    dq, *dkvs = attend_back(
        table, q, kvs, [a.reshape(2, 2, 64, 128) for a in grad_att], attT, lse
    )
    dkvs = [a.reshape(ROWS, 128) for a in after(tuple(dkvs), *branches[1:])]
    dkvs = dkvs[:1] + [ring(dkvs[k], "cp_1", 4 - k) for k in (1, 2, 3)]
    b_own = jnp.concatenate(after(branches, dq), axis=0)
    b_other = sibling(b_own)
    came = [ring(after(mixes[1], dq), "sp_0", 3)]
    came += [ring(after(mixes[k], *dkvs[1:]), "sp_0", 4 - k) for k in (2, 3)]
    gw_cols, gw_down = sum_units(gw_units)
    graw, line = heads_back(
        dq.reshape(ROWS, 128), dkvs, raw, cosine, sine, gq, gk, normed, att, b_own, b_other,
        (gw_cols,),
    )
    terms = jnp.sum(exchange(line, DC).astype(F32), axis=0)
    lasts = sum_cores(*rows_back(graw, x_own, x_other, gain_attn, lines, tuple(came)))
    lasts = [lasts[0]] + [a.astype(BF) for a in lasts[1:]]
    packed = pack_grads(terms, gw_cols)
    cols = exchange(packed, SP)
    last = grad_middle + lasts[0]
    mixed = mixes[0] + sum(a.astype(F32) for a in came)
    came = [ring(lasts[k], "sp_0", 4 - k) for k in (1, 2, 3)]
    last += sum(a.astype(F32) for a in after(came, packed))
    rows = jnp.stack([last, mixed]).astype(BF).reshape(2, 2, 64, D).swapaxes(0, 1)
    rows = own_first(jnp.stack([rows[0], pair(rows[1], "cp_0")]), half)
    grad_tokens, mixed = rows[:, 0], rows[:, 1]

    back = [(d, s) for s, d in perm]
    gw_out = jnp.concatenate([terms[r : r + 8] for r in range(72, 104, 8)], axis=1)
    downs = lax.ppermute(jnp.concatenate([gw_out, gw_down], axis=0), DP_CP_SP, back)
    downs = after(downs, rows)
    grad_w_out, grad_w_down = downs[:8], downs[8:]
    weights = (w_query, w_key, w_value, w_gate, w_up)
    gains = (attn_gain[None], ffn_gain[None])
    *grads, grad_attn_gain, grad_ffn_gain, heads = unpack_grads(cols, weights, gains)
    grad_w_query, grad_w_key, grad_w_value, grad_w_gate, grad_w_up = grads
    return (
        mixed,
        grad_tokens,
        grad_attn_gain[0],
        grad_ffn_gain[0],
        heads,
        grad_w_query,
        grad_w_key,
        grad_w_value,
        grad_w_out,
        grad_w_gate,
        grad_w_up,
        grad_w_down,
    )


def solution(mesh):
    torus = Mesh(
        mesh.devices.reshape(mesh.shape["dp"], 2, 4, 4, 2), ("dp", "cp_0", "cp_1", "sp_0", "sp_1")
    )
    rows, split = P("dp", CP_SP, None), P(DP_CP_SP, None)
    in_specs = (rows, rows, P(), P(DP_CP_SP), P(DP_CP_SP), P()) + (split,) * 7
    out_specs = (rows, rows, P(DP_CP_SP), P(DP_CP_SP), P()) + (split,) * 7
    return jax.shard_map(
        on_device, mesh=torus, in_specs=in_specs, out_specs=out_specs, check_vma=False
    )
```

```python
from functools import partial

import jax
import jax.numpy as jnp
from jax import lax
from jax.experimental import pallas as pl
from jax.experimental.pallas import tpu as pltpu
from jax.sharding import Mesh
from jax.sharding import PartitionSpec as P

SP = ("sp_0", "sp_1")
DC = ("dp", "cp_0", "cp_1")
DP_CP_SP = ("dp", "cp_0", "cp_1", "sp_0", "sp_1")
CP_SP = ("cp_0", "cp_1", "sp_0", "sp_1")

EPSILON = 1e-05
ROPE_BASE = 1000000.0
BF = jnp.bfloat16
F32 = jnp.float32

D = 1024
HD = 64
FF = 4608
FS = FF // 8
FP = 640
BLK = 256
ROWS = 1024
TILE = 256
VMEM_LIMIT = 56 * 1024 * 1024


def dot(left, right):
    return jnp.dot(left, right, preferred_element_type=F32)


def dot_rows(left, right):
    return lax.dot_general(left, right, (((0,), (0,)), ((), ())), preferred_element_type=F32)


def dot_cols(left, right):
    return lax.dot_general(left, right, (((1,), (1,)), ((), ())), preferred_element_type=F32)


def call(body, out, **kw):
    flops = kw.pop("flops", 0)
    nbytes = kw.pop("nbytes", 0)
    after = kw.pop("after", ())
    if after:
        inner, count = body, len(after)
        kw["in_specs"] = [pl.BlockSpec(memory_space=pl.ANY)] * count + list(kw["in_specs"])

        def body(*refs):
            return inner(*refs[count:])

        return partial(call(body, out, flops=flops, nbytes=nbytes, **kw), *after)
    return pl.pallas_call(
        body,
        out_shape=out,
        compiler_params=pltpu.CompilerParams(vmem_limit_bytes=VMEM_LIMIT),
        cost_estimate=pl.CostEstimate(flops=flops, bytes_accessed=nbytes, transcendentals=0),
        **kw,
    )


def shaped(shape, dtype):
    return jax.ShapeDtypeStruct(shape, dtype)


def ring(x, axis, k):
    return lax.ppermute(x, axis, [(i, (i + k) % 4) for i in range(4)])


def pair(x, axis):
    return lax.ppermute(x, axis, [(0, 1), (1, 0)])


def sibling(x):
    return pair(x, "sp_1")


def exchange(x, axis):
    return lax.all_to_all(x, axis, 0, 0, tiled=True)


def after(x, *first):
    return lax.optimization_barrier((x, *first))[0]


def around(x, axis):
    return [x] + [ring(x, axis, k) for k in (1, 2, 3)]


def own_first(both, half):
    return jnp.where(half == 0, both, both[::-1])


def swapped(rows):
    return jnp.concatenate([rows[0], pair(rows[1], "cp_0")], axis=0)


def sum_cores(own, other):
    came = sibling(other)
    return [
        own[r : r + 128].astype(F32) + came[r : r + 128].astype(F32) for r in range(0, 512, 128)
    ]


def rms_of(x):
    return lax.rsqrt(jnp.mean(x * x, axis=-1, keepdims=True) + EPSILON)


def norm_back(x, gain, upstream):
    r = rms_of(x)
    n = x * r
    scaled = upstream * gain
    return r * (scaled - n * jnp.mean(scaled * n, axis=-1, keepdims=True))


def low_half(shape):
    return lax.broadcasted_iota(jnp.int32, shape, 1) < HD


def head_mean(v):
    low = low_half(v.shape)
    first = jnp.sum(jnp.where(low, v, 0.0), axis=1, keepdims=True)
    second = jnp.sum(jnp.where(low, 0.0, v), axis=1, keepdims=True)
    return jnp.where(low, first, second) * (1.0 / HD)


def swap_halves(v):
    lane = lax.broadcasted_iota(jnp.int32, v.shape, 1)
    return jnp.where(lane % HD < HD // 2, pltpu.roll(v, 96, 1), pltpu.roll(v, 32, 1))


def row_tables(block_of, core, half, cycle, level):
    slots = jnp.arange(16, dtype=jnp.int32)
    blocks = block_of.reshape(2, 4, 2)
    blocks = jnp.where(half == 0, blocks, blocks[::-1])
    local = lax.dynamic_index_in_dim(blocks, cycle, 1, keepdims=False)
    z = (level - jnp.arange(4, dtype=jnp.int32)) % 4
    pick = (z // 2)[None, :] == 1
    by_z = jnp.where(pick, local[:, 1:], local[:, :1]).T
    entries = HD // 2
    inverse = ROPE_BASE ** (-(2.0 * jnp.arange(entries, dtype=F32)) / HD)
    inverse = jnp.tile(inverse, 4)
    sign = jnp.tile(jnp.concatenate([-jnp.ones(entries, F32), jnp.ones(entries, F32)]), 2)
    first = (by_z.reshape(8) * BLK).astype(F32)[:, None] * inverse[None]
    rel = jnp.arange(2, dtype=jnp.int32)[:, None, None]
    row = jnp.arange(64, dtype=jnp.int32)[None, None, :]
    inner = ((z % 2)[None, :, None] * 128 + (rel ^ core) * 64 + row).reshape(512)
    inner = inner.astype(F32)[:, None] * inverse[None]
    ca, sa = (f(first).reshape(1, 4, 2, 1, 128) for f in (jnp.cos, jnp.sin))
    cb, sb = (f(inner).reshape(2, 4, 1, 64, 128) for f in (jnp.cos, jnp.sin))
    cosine = (ca * cb - sa * sb).reshape(ROWS, 128)
    sine = ((sa * cb + ca * sb) * sign).reshape(ROWS, 128)
    distance = (cycle - (slots >> 1)) & 3
    at = distance * 4 + ((slots >> 3) ^ half) * 2 + (slots & 1)
    slot_at = jnp.sum(jnp.where(block_of[None, :] == slots[:, None], at[None, :], 0), axis=1)
    place = (level - jnp.arange(4, dtype=jnp.int32)) & 3
    table = jnp.concatenate([local.reshape(4), place, slot_at, core[None]]).astype(jnp.int32)
    return cosine, sine, table


def project_body(own_ref, other_ref, gain_ref, w_ref, cos_ref, sin_ref, gq_ref, gk_ref, n_ref, raw_ref, q_ref, kv_ref):
    x = picked(own_ref, other_ref).astype(F32)
    normed = (x * rms_of(x) * gain_ref[...].astype(F32)).astype(BF)
    n_ref[...] = normed
    raw = dot(normed, w_ref[:, :64].reshape(D, 256))
    raw_ref[...] = raw
    cosine, sine = cos_ref[...], sin_ref[...]

    def turned(v, gain):
        v = v * lax.rsqrt(head_mean(v * v) + EPSILON) * gain
        return (v * cosine + swap_halves(v) * sine).astype(BF)

    q_ref[...] = turned(raw[:, :128], gq_ref[...]) * jnp.asarray(0.125, BF)
    right = raw[:, 128:]
    kv_ref[...] = jnp.where(low_half(right.shape), turned(right, gk_ref[...]), right.astype(BF))


def picked(own_ref, other_ref):
    return jnp.where(pl.program_id(0) < 2, own_ref[...], other_ref[...])


def halves(width):
    return [
        pl.BlockSpec((TILE, width), lambda t: (jnp.minimum(t, 1), 0)),
        pl.BlockSpec((TILE, width), lambda t: (jnp.maximum(t - 2, 0), 0)),
    ]


def tiles(width):
    return pl.BlockSpec((TILE, width), lambda t: (t, 0))


def whole(*shape):
    return pl.BlockSpec(shape, lambda t: (0,) * len(shape))


def project(x, other, gain, w, cosine, sine, gq, gk, after):
    return call(
        project_body,
        (
            shaped((ROWS, D), BF),
            shaped((ROWS, 256), F32),
            shaped((ROWS, 128), BF),
            shaped((ROWS, 128), BF),
        ),
        grid=(ROWS // TILE,),
        in_specs=halves(D) + [whole(1, D), whole(16, 264, 256), tiles(128), tiles(128), whole(1, 128), whole(1, 128)],
        out_specs=(tiles(D), tiles(256), tiles(128), tiles(128)),
        flops=2 * ROWS * D * 256,
        nbytes=7 * 2**20,
        after=after,
        name="project",
    )(x, other, gain, w, cosine, sine, gq, gk)


def heads_back_body(
    dq_ref, k0_ref, k1_ref, k2_ref, k3_ref, raw_ref, cos_ref, sin_ref, gq_ref, gk_ref, n_ref,
    att_ref, own_ref, other_ref, graw_ref, line_ref, gw_acc, out_acc, head_acc,
):
    step = pl.program_id(0)

    @pl.when(step == 0)
    def _():
        gw_acc[...] = jnp.zeros_like(gw_acc)
        out_acc[...] = jnp.zeros_like(out_acc)
        head_acc[...] = jnp.zeros_like(head_acc)

    cosine, sine = cos_ref[...], sin_ref[...]

    def back(raw, grad, gain):
        r = lax.rsqrt(head_mean(raw * raw) + EPSILON)
        n = raw * r
        up = grad * cosine + swap_halves(grad * sine)
        scaled = up * gain
        return r * (scaled - n * head_mean(scaled * n)), jnp.sum(up * n, axis=0, keepdims=True)

    raw = raw_ref[...]
    graw_q, gain_q = back(raw[:, :128], dq_ref[...], gq_ref[...])
    dkv = (k0_ref[...].astype(F32) + k1_ref[...].astype(F32)) + (
        k2_ref[...].astype(F32) + k3_ref[...].astype(F32)
    )
    graw_k, gain_k = back(raw[:, 128:], dkv, gk_ref[...])
    gain_k = jnp.where(low_half(gain_k.shape), gain_k, 0.0)
    head_acc[...] += jnp.concatenate([gain_q, gain_k], axis=1)
    graw = jnp.concatenate([graw_q, jnp.where(low_half(dkv.shape), graw_k, dkv)], axis=1).astype(BF)
    graw_ref[...] = graw
    gw_acc[...] += dot_rows(n_ref[...], graw)
    out_acc[...] += dot_rows(att_ref[...], picked(own_ref, other_ref))

    @pl.when(step == pl.num_programs(0) - 1)
    def _():
        heads = jnp.broadcast_to(head_acc[...], (8, 256))
        for k in range(16):
            rows = out_acc[8 * k : 8 * k + 8]
            parts = [gw_acc[64 * k : 64 * k + 64], heads]
            parts += [rows[:, c : c + 256] for c in range(0, D, 256)]
            line_ref[k] = jnp.concatenate(parts, axis=0).astype(BF)


def heads_back(dq, dkvs, raw, cosine, sine, gq, gk, normed, att, b_own, b_other, after):
    return call(
        heads_back_body,
        (shaped((ROWS, 256), BF), shaped((16, 104, 256), BF)),
        grid=(ROWS // TILE,),
        in_specs=[tiles(128)] * 5
        + [tiles(256), tiles(128), tiles(128), whole(1, 128), whole(1, 128), tiles(D), tiles(128)]
        + halves(D),
        out_specs=(tiles(256), whole(16, 104, 256)),
        scratch_shapes=[
            pltpu.VMEM((D, 256), F32),
            pltpu.VMEM((128, D), F32),
            pltpu.VMEM((1, 256), F32),
        ],
        flops=2 * ROWS * D * 384,
        nbytes=10 * 2**20,
        after=after,
        name="heads_back",
    )(dq, *dkvs, raw, cosine, sine, gq, gk, normed, att, b_own, b_other)


def rows_back_body(graw_ref, own_ref, other_ref, gain_ref, w_ref, out_own, out_other):
    x = picked(own_ref, other_ref).astype(F32)
    grad = dot_cols(graw_ref[...], w_ref[:, :64].reshape(D, 256))
    part = norm_back(x, gain_ref[...].astype(F32), grad).astype(BF)

    @pl.when(pl.program_id(0) < 2)
    def _():
        out_own[...] = part

    @pl.when(pl.program_id(0) >= 2)
    def _():
        out_other[...] = part


def rows_back(graw, x, other, gain, w, after):
    return call(
        rows_back_body,
        (shaped((ROWS // 2, D), BF),) * 2,
        grid=(ROWS // TILE,),
        in_specs=[tiles(256)] + halves(D) + [whole(1, D), whole(16, 264, 256)],
        out_specs=tuple(halves(D)),
        flops=2 * ROWS * D * 256,
        nbytes=5 * 2**20,
        after=after,
        name="rows_back",
    )(graw, x, other, gain, w)


def stored(tab_ref, ref, half, h):
    return jnp.concatenate(
        [ref[c, tab_ref[4 + 2 * h + zz], half] for c in range(2) for zz in range(2)], axis=0
    )


def store(tab_ref, ref, half, h, block):
    for c in range(2):
        for zz in range(2):
            row = (c * 2 + zz) * 64
            ref[c, tab_ref[4 + 2 * h + zz], half] = block[row : row + 64]


def heads_across(block):
    flat = block.astype(F32).T
    return jnp.concatenate([flat[:HD], flat[HD:]], axis=1)


def diagonal_mask(core):
    def place(t):
        return ((t >> 6) & 1) * 128 + ((t >> 7) ^ core) * 64 + (t & 63)

    keys = place(lax.broadcasted_iota(jnp.int32, (BLK, 2 * BLK), 0))
    queries = place(lax.broadcasted_iota(jnp.int32, (BLK, 2 * BLK), 1) & 255)
    return keys <= queries


def pair_at(tab_ref, i, o):
    count = tab_ref[2 * o]
    first = i < count
    qb = 2 * o + jnp.where(first, 0, 1)
    slot = tab_ref[8 + jnp.where(first, i, i - count)]
    return qb, slot


def attend_body(tab_ref, q_ref, kv0, kv1, kv2, kv3, att_ref, attT_ref, lse_ref, qT, kv, vT, acc):
    zeros = jnp.zeros((HD, 2 * BLK), BF)
    for qb in range(4):
        qT[qb, :HD] = heads_across(stored(tab_ref, q_ref, qb // 2, qb % 2)).astype(BF)
        qT[qb, HD:] = zeros
    for slot in range(16):
        block = stored(tab_ref, (kv0, kv1, kv2, kv3)[slot // 4], (slot >> 1) & 1, slot & 1)
        kv[slot] = block
        flat = block.astype(F32).T
        vT[slot] = jnp.concatenate([jnp.ones((16, BLK), F32), flat[HD:]], axis=0).astype(BF)
    acc[...] = jnp.zeros_like(acc)

    def pair(qb, slot, mask=None):
        p = jnp.exp(dot(kv[slot], qT[qb]))
        if mask is not None:
            p = jnp.where(mask, p, 0.0)
        acc[qb] += dot(vT[slot], p.astype(BF))

    def step(i, carry):
        for o in range(2):
            pair(*pair_at(tab_ref, i, o))
        return carry

    lax.fori_loop(0, 15, step, 0, unroll=15)
    mask = diagonal_mask(tab_ref[24])
    for qb in range(4):
        pair(qb, tab_ref[8 + tab_ref[qb]], mask)
        total = acc[qb, :1]
        out = acc[qb, 16:] / total
        flat = jnp.concatenate([out[:, :BLK], out[:, BLK:]], axis=0)
        attT_ref[qb] = flat
        lse_ref[qb] = jnp.log(total)
        store(tab_ref, att_ref, qb // 2, qb % 2, flat.T.astype(BF))


def in_smem():
    return pl.BlockSpec(memory_space=pltpu.SMEM)


def in_vmem():
    return pl.BlockSpec(memory_space=pltpu.VMEM)


def attend(table, q, kvs, after):
    return call(
        attend_body,
        (
            shaped((2, 4, 2, 64, 128), BF),
            shaped((4, 128, BLK), F32),
            shaped((4, 1, 2 * BLK), F32),
        ),
        in_specs=[in_smem()] + [in_vmem()] * 5,
        out_specs=(in_vmem(), in_vmem(), in_vmem()),
        scratch_shapes=[
            pltpu.VMEM((4, 128, 2 * BLK), BF),
            pltpu.VMEM((16, BLK, 128), BF),
            pltpu.VMEM((16, HD + 16, BLK), BF),
            pltpu.VMEM((4, HD + 16, 2 * BLK), F32),
        ],
        flops=34 * 4 * BLK * 2 * BLK * 128,
        nbytes=2 * 2**20,
        after=after,
        name="attend",
    )(table, q, *kvs)


def attend_back_body(
    tab_ref, q_ref, kv0, kv1, kv2, kv3, g0, g1, g2, g3, attT_ref, lse_ref,
    dq_ref, dkv0, dkv1, dkv2, dkv3, g_ref, qT, gT, qn, gn, kv, kT, delta, dqT, dkv,
):
    for k, ref in enumerate((g0, g1, g2, g3)):
        g_ref[0, k], g_ref[1, k] = ref[0], ref[1]
    zeros = jnp.zeros((HD, 2 * BLK), F32)
    for qb in range(4):
        across = jnp.concatenate([heads_across(stored(tab_ref, q_ref, qb // 2, qb % 2)), zeros], axis=0)
        qT[qb] = across.astype(BF)
        qn[qb] = across.T.astype(BF)
        g_across = heads_across(stored(tab_ref, g_ref, qb // 2, qb % 2))
        out = attT_ref[qb]
        out = jnp.concatenate([out[:HD], out[HD:]], axis=1)
        delta[qb] = jnp.sum(g_across * out, axis=0, keepdims=True)
        g_across = jnp.concatenate([zeros, g_across], axis=0)
        gT[qb] = g_across.astype(BF)
        gn[qb] = g_across.T.astype(BF)
    for slot in range(16):
        block = stored(tab_ref, (kv0, kv1, kv2, kv3)[slot // 4], (slot >> 1) & 1, slot & 1)
        kv[slot] = block
        kT[slot] = block.astype(F32).T[:HD].astype(BF)
    dqT[...] = jnp.zeros_like(dqT)
    dkv[...] = jnp.zeros_like(dkv)

    def pair(qb, slot, mask=None):
        keys = kv[slot]
        p = jnp.exp(dot(keys, qT[qb]) - lse_ref[qb])
        if mask is not None:
            p = jnp.where(mask, p, 0.0)
        ds = (p * (dot(keys, gT[qb]) - delta[qb])).astype(BF)
        dkv[slot] += dot(ds, qn[qb]) + dot(p.astype(BF), gn[qb])
        dqT[qb] += dot(kT[slot], ds)

    def step(i, carry):
        for o in range(2):
            pair(*pair_at(tab_ref, i, o))
        return carry

    lax.fori_loop(0, 15, step, 0, unroll=15)
    mask = diagonal_mask(tab_ref[24])
    for qb in range(4):
        pair(qb, tab_ref[8 + tab_ref[qb]], mask)
        flat = jnp.concatenate([dqT[qb, :, :BLK], dqT[qb, :, BLK:]], axis=0)
        store(tab_ref, dq_ref, qb // 2, qb % 2, flat.T * 0.125)
    for slot in range(16):
        out = (dkv0, dkv1, dkv2, dkv3)[slot // 4]
        store(tab_ref, out, (slot >> 1) & 1, slot & 1, dkv[slot].astype(BF))


def attend_back(table, q, kvs, gs, attT, lse):
    return call(
        attend_back_body,
        (shaped((2, 4, 2, 64, 128), F32),) + (shaped((2, 4, 2, 64, 128), BF),) * 4,
        in_specs=[in_smem()] + [in_vmem()] * 11,
        out_specs=(in_vmem(),) * 5,
        scratch_shapes=[
            pltpu.VMEM((2, 4, 2, 64, 128), BF),
            pltpu.VMEM((4, 128, 2 * BLK), BF),
            pltpu.VMEM((4, 128, 2 * BLK), BF),
            pltpu.VMEM((4, 2 * BLK, 128), BF),
            pltpu.VMEM((4, 2 * BLK, 128), BF),
            pltpu.VMEM((16, BLK, 128), BF),
            pltpu.VMEM((16, HD, BLK), BF),
            pltpu.VMEM((4, 1, 2 * BLK), F32),
            pltpu.VMEM((4, HD, 2 * BLK), F32),
            pltpu.VMEM((16, BLK, 128), F32),
        ],
        flops=34 * 10 * BLK * 2 * BLK * 128,
        nbytes=4 * 2**20,
        name="attend_back",
    )(table, q, *kvs, *gs, attT, lse)


def ffn_body(
    a0, a1, a2, a3, b0, b1, b2, b3, x_own, x_other, g_own, g_other, gain_ref,
    wo_own, wo_other, units_ref, lines_ref,
    mixed_own, mixed_other, part_own, part_other, gw_ref, wd, n_all, p_all, h_all,
):
    step = pl.program_id(0)

    @pl.when(step == 0)
    def _():
        rows = []
        for k in range(16):
            parts = [lines_ref[k, r : r + 40].astype(F32)[:36] for r in range(104, 264, 40)]
            rows.append(jnp.concatenate(parts, axis=1))
        rows.append(jnp.zeros((FP - FS, D), F32))
        wd[...] = jnp.concatenate(rows, axis=0).astype(BF)

    core, first = step // 2, step % 2 * 2
    middle = picked(x_own, x_other).astype(F32)
    for c, (refs, w_ref) in enumerate((((a0, a1, a2, a3), wo_own), ((b0, b1, b2, b3), wo_other))):
        pieces = []
        for k, ref in enumerate(refs):
            at = [(core ^ c) * 512 + ((first + j - k) & 3) * 128 for j in range(2)]
            pieces.append(jnp.concatenate([ref[pl.ds(r, 128)] for r in at], axis=0))
        middle += dot(jnp.concatenate(pieces, axis=1), w_ref[...])
    gain = gain_ref[...].astype(F32)
    normed = (middle * rms_of(middle) * gain).astype(BF)
    wgu = units_ref[...].reshape(D, 2 * FP)
    pre = dot(normed, wgu)
    gate, up = pre[:, :FP], pre[:, FP:]
    s = 1.0 / (1.0 + jnp.exp(-gate))
    act = gate * s
    hidden = (act * up).astype(BF)
    row = lax.broadcasted_iota(jnp.int32, (TILE, 1), 0)
    here = jnp.logical_and(step == 0, row < 128)
    mixed = (dot(hidden, wd[...]) + jnp.where(here, middle, 0.0)).astype(BF)
    r = pl.ds(pl.multiple_of(step % 2 * TILE, TILE), TILE)
    g = jnp.where(step < 2, g_own[r], g_other[r])
    gh = dot_cols(g, wd[...])
    at = pl.ds(pl.multiple_of(step * TILE, TILE), TILE)
    h_all[at], n_all[at] = hidden, normed
    gpre = jnp.concatenate([gh * up * s * (1.0 + gate * (1.0 - s)), gh * act], axis=1).astype(BF)
    p_all[at] = gpre
    part = norm_back(middle, gain, dot_cols(gpre, wgu)).astype(BF)

    @pl.when(step < 2)
    def _():
        mixed_own[...] = mixed
        part_own[...] = part

    @pl.when(step >= 2)
    def _():
        mixed_other[...] = mixed
        part_other[...] = part

    @pl.when(step == pl.num_programs(0) - 1)
    def _():
        for k in range(4):
            cols = dot_rows(n_all[:, 256 * k : 256 * k + 256], p_all[...])
            for j in range(4):
                gw_ref[4 * k + j, :64] = cols[64 * j : 64 * j + 64].astype(BF)
        h = h_all[...]
        downs = dot_rows(h[:512], g_own[...]) + dot_rows(h[512:], g_other[...])
        for k in range(16):
            rows = jnp.concatenate([downs[36 * k : 36 * k + 36], jnp.zeros((4, D), F32)], axis=0)
            rows = jnp.concatenate([rows, jnp.zeros((40, 2 * FP - D), F32)], axis=1)
            gw_ref[k, 64:] = rows.astype(BF)


def ffn(own, other, x, g, gain, wo, units, lines):
    return call(
        ffn_body,
        (shaped((ROWS // 2, D), BF),) * 4 + (shaped((16, 104, 2 * FP), BF),),
        grid=(ROWS // TILE,),
        in_specs=[whole(ROWS, 128)] * 8
        + halves(D)
        + [whole(ROWS // 2, D)] * 2
        + [whole(1, D), whole(D // 2, D), whole(D // 2, D)]
        + [whole(16, 64, 2 * FP), whole(16, 264, 256)],
        out_specs=tuple(halves(D) * 2) + (whole(16, 104, 2 * FP),),
        scratch_shapes=[
            pltpu.VMEM((FP, D), BF),
            pltpu.VMEM((ROWS, D), BF),
            pltpu.VMEM((ROWS, 2 * FP), BF),
            pltpu.VMEM((ROWS, FP), BF),
        ],
        flops=2 * ROWS * D * (D + 9 * FP),
        nbytes=24 * 2**20,
        name="ffn",
    )(*own, *other, *x, *g, gain, *wo, units, lines)


def branch_body(g_ref, t0, t1, t2, t3, wo_own, wo_other, mid_ref, branch_ref, own_ref, other_ref):
    total = g_ref[...].astype(F32) + t0[...] + t1[...].astype(F32)
    total += t2[...].astype(F32) + t3[...].astype(F32)
    mid_ref[...] = total
    branch = total.astype(BF)
    branch_ref[...] = branch
    for w_ref, out_ref in ((wo_own, own_ref), (wo_other, other_ref)):
        grad = dot_cols(branch, w_ref[...]).astype(BF)
        for k in range(4):
            at = (-k) % 4 * 128
            out_ref[k] = grad[:, at : at + 128]


def branch_of(g_rows, terms, wo):
    return call(
        branch_body,
        (shaped((128, D), F32), shaped((128, D), BF)) + (shaped((4, 128, 128), BF),) * 2,
        in_specs=[in_vmem()] * 7,
        out_specs=(in_vmem(),) * 4,
        flops=2 * 128 * D * D,
        nbytes=4 * 2**20,
        name="branch",
    )(g_rows, *terms, *wo)


def columns_body(wq, wk, wv, wg, wu, gains_ref, out_ref):
    wq, wk, wv, wg, wu = (w[...].astype(F32) for w in (wq, wk, wv, wg, wu))
    gains = jnp.concatenate([gains_ref[...].astype(F32), jnp.zeros((8, 2 * FP), F32)], axis=1)
    gap = jnp.zeros((8, FP - FS), F32)
    for s in range(8):
        parts = [w[:, s * n : s * n + n] for w, n in ((wq, 128), (wk, HD), (wv, HD))]
        parts += [wg[:, s * FS : s * FS + FS], gap, wu[:, s * FS : s * FS + FS], gap]
        out_ref[s] = jnp.concatenate([jnp.concatenate(parts, axis=1), gains], axis=0).astype(BF)


def pack_columns(weights, gains):
    return call(
        columns_body,
        shaped((8, 16, 256 + 2 * FP), BF),
        in_specs=[in_vmem()] * 6,
        out_specs=in_vmem(),
        nbytes=2**20,
        name="pack_columns",
    )(*weights, gains)


def lines_body(cols_ref, downs_ref, out_ref):
    gains = cols_ref[0, :, :256].astype(F32)[8:]
    for s in range(1, 8):
        gains += cols_ref[s, :, :256].astype(F32)[8:]
    downs = downs_ref[...].astype(F32)
    outs, downs = downs[:8], jnp.concatenate([downs[8:], jnp.zeros((4, D), F32)], axis=0)
    parts = [cols_ref[s, :, :256].astype(F32)[:8] for s in range(8)] + [gains]
    parts += [outs[:, c : c + 256] for c in range(0, D, 256)]
    parts += [downs[:, c : c + 256] for c in range(0, D, 256)]
    line = jnp.concatenate(parts, axis=0).astype(BF)
    for k in range(16):
        out_ref[k] = line


def pack_lines(cols, downs, after):
    return call(
        lines_body,
        shaped((16, 264, 256), BF),
        in_specs=[in_vmem()] * 2,
        out_specs=in_vmem(),
        nbytes=3 * 2**20,
        after=after,
        name="pack_lines",
    )(cols, downs)


def units_body(cols_ref, out_ref):
    rows = [cols_ref[s, :, 256:].astype(F32)[:8] for s in range(8)]
    unit = jnp.concatenate(rows, axis=0).astype(BF)
    for k in range(16):
        out_ref[k] = unit


def pack_units(cols):
    return call(
        units_body,
        shaped((16, 64, 2 * FP), BF),
        in_specs=[in_vmem()],
        out_specs=in_vmem(),
        nbytes=3 * 2**20,
        name="pack_units",
    )(cols)


def sum_units_body(in_ref, cols_ref, down_ref):
    total = in_ref[0].astype(F32)
    for k in range(1, 16):
        total += in_ref[k].astype(F32)
    cols_ref[...] = total[:64]
    down_ref[...] = total[64:100, :D]


def sum_units(terms):
    return call(
        sum_units_body,
        (shaped((64, 2 * FP), F32), shaped((36, D), F32)),
        in_specs=[in_vmem()],
        out_specs=(in_vmem(),) * 2,
        nbytes=5 * 2**20,
        name="sum_units",
    )(terms)


def grads_body(lines_ref, units_ref, out_ref):
    heads = jnp.concatenate([lines_ref[64:72], jnp.zeros((8, 2 * FP), F32)], axis=1)
    for s in range(8):
        rows = slice(8 * s, 8 * s + 8)
        grads = jnp.concatenate([lines_ref[rows], units_ref[rows]], axis=1)
        out_ref[s] = jnp.concatenate([grads, heads], axis=0).astype(BF)


def pack_grads(lines, units):
    return call(
        grads_body,
        shaped((8, 16, 256 + 2 * FP), BF),
        in_specs=[in_vmem()] * 2,
        out_specs=in_vmem(),
        nbytes=2**20,
        name="pack_grads",
    )(lines, units)


def unpack_body(
    in_ref, wq, wk, wv, wg, wu, gain_attn, gain_ffn,
    gq_ref, gk_ref, gv_ref, gg_ref, gu_ref, attn_ref, ffn_ref, head_ref,
):
    blocks = [in_ref[s].astype(F32) for s in range(8)]

    def taken(w_ref, g_ref, at, n):
        grad = jnp.concatenate([b[:8, at : at + n] for b in blocks], axis=1)
        g_ref[...] = grad
        return jnp.sum(w_ref[...].astype(F32) * grad, axis=1, keepdims=True)

    attn = taken(wq, gq_ref, 0, 128) + taken(wk, gk_ref, 128, HD) + taken(wv, gv_ref, 192, HD)
    def across(column):
        lane = lax.broadcasted_iota(jnp.int32, (8, 8), 1)
        row = lax.broadcasted_iota(jnp.int32, (8, 8), 0)
        return jnp.sum(jnp.where(lane == row, column, 0.0), axis=0, keepdims=True)

    attn_ref[...] = across(attn) / gain_attn[...].astype(F32)
    feed = taken(wg, gg_ref, 256, FS) + taken(wu, gu_ref, 256 + FP, FS)
    ffn_ref[...] = across(feed) / gain_ffn[...].astype(F32)
    heads = blocks[0][8:, :256]
    for b in blocks[1:]:
        heads += b[8:, :256]
    head_ref[0:1] = heads[:1, :HD] + heads[:1, HD : 2 * HD]
    head_ref[1:2] = heads[:1, 2 * HD : 3 * HD]


def unpack_grads(cols, weights, gains):
    return call(
        unpack_body,
        tuple(shaped(w.shape, F32) for w in weights)
        + (shaped((1, 8), F32), shaped((1, 8), F32), shaped((2, HD), F32)),
        in_specs=[in_vmem()] * 8,
        out_specs=(in_vmem(),) * 8,
        nbytes=2**20,
        name="unpack_grads",
    )(cols, *weights, *gains)


def on_device(
    tokens, cotangent, block_of, attn_gain, ffn_gain, head_gains,
    w_query, w_key, w_value, w_out, w_gate, w_up, w_down,
):
    core, level = lax.axis_index("sp_1"), lax.axis_index("sp_0")
    cycle, half = lax.axis_index("cp_1"), lax.axis_index("cp_0")
    gains_f = head_gains.astype(F32)
    gq = jnp.tile(gains_f[0], 2)[None]
    gk = jnp.tile(gains_f[1], 2)[None]
    cosine, sine, table = row_tables(block_of, core, half, cycle, level)

    place = jnp.arange(8)[:, None] == lax.axis_index(SP)
    gains = jnp.stack([attn_gain, ffn_gain])[:, None, :]
    gains = jnp.where(place[None], gains, jnp.zeros((), BF)).reshape(1, 128)
    gains = jnp.pad(gains, ((0, 7), (0, 128)))
    rows = own_first(jnp.stack([tokens, cotangent], axis=1), half)
    rows = jnp.stack([rows[0], pair(rows[1], "cp_0")], axis=1).reshape(2, 128, D)
    columns = pack_columns((w_query, w_key, w_value, w_gate, w_up), gains)
    cols = exchange(columns, SP)
    perm = [(d, (d % 16) * 8 + d // 16) for d in range(128)]
    downs = lax.ppermute(jnp.concatenate([w_out, w_down], axis=0), DP_CP_SP, perm)
    line = pack_lines(cols, downs, (rows,))
    lines = exchange(line, DC)
    gains = lines[:, 64, :128]
    gain_attn, gain_ffn = gains[:, :64].reshape(1, D), gains[:, 64:].reshape(1, D)

    both = around(after(rows, line).reshape(256, D), "sp_0")
    x_own = jnp.concatenate([a[:128] for a in both], axis=0)
    g_own = jnp.concatenate([a[128:] for a in both], axis=0)
    x_other = sibling(x_own)
    g_rows = rows[1]

    units = pack_units(after(cols, line))
    normed, raw, q, kv = project(
        x_own, x_other, gain_attn, lines, cosine, sine, gq, gk, (units,)
    )
    kvs = around(kv, "cp_1")
    units = exchange(after(units, *kvs[1:]), DC)
    g_other = sibling(after(g_own, q))
    wo_rows = jnp.concatenate([lines[:, r : r + 8] for r in range(72, 104, 8)], axis=2)
    wo_own = jnp.concatenate(around(after(wo_rows, *kvs[1:]).reshape(128, D), "sp_0"), axis=0)
    kvs = [a.reshape(2, 4, 2, 64, 128) for a in kvs]
    q = q.reshape(2, 4, 2, 64, 128)
    att, attT, lse = attend(table, q, kvs, ())
    att = att.reshape(ROWS, 128)
    wo = (wo_own, sibling(after(wo_own, att)))
    own = around(att, "sp_0")
    other = [sibling(a) for a in own]
    mixed_own, mixed_other, part_own, part_other, gw_units = ffn(
        own, other, (x_own, x_other), (g_own, g_other), gain_ffn, wo, units, lines
    )

    mids = sum_cores(part_own, part_other)
    terms = [ring(mids[k].astype(BF), "sp_0", 4 - k) for k in (1, 2, 3)]
    gw_units = exchange(gw_units, DC)
    mids = mids[:1] + terms
    grad_middle, branch, for_own, for_other = branch_of(g_rows, mids, wo)
    mixes = sum_cores(mixed_own, after(mixed_other, mids[0]))
    mixes = mixes[:1] + [a.astype(BF) for a in mixes[1:]]
    grad_att = jnp.stack([for_own, sibling(for_other)], axis=1)
    grad_att, *mixes = lax.optimization_barrier((grad_att, *mixes))
    grad_att = [grad_att[0]] + [ring(grad_att[k], "sp_0", k) for k in (1, 2, 3)]
    branch, *mixes = after((branch, *mixes), *grad_att)
    branches = around(branch, "sp_0")
    dq, *dkvs = attend_back(
        table, q, kvs, [a.reshape(2, 2, 64, 128) for a in grad_att], attT, lse
    )
    dkvs = [a.reshape(ROWS, 128) for a in after(tuple(dkvs), *branches[1:])]
    dkvs = dkvs[:1] + [ring(dkvs[k], "cp_1", 4 - k) for k in (1, 2, 3)]
    b_own = jnp.concatenate(after(branches, dq), axis=0)
    b_other = sibling(b_own)
    came = [ring(after(mixes[1], dq), "sp_0", 3)]
    came += [ring(after(mixes[k], *dkvs[1:]), "sp_0", 4 - k) for k in (2, 3)]
    gw_cols, gw_down = sum_units(gw_units)
    graw, line = heads_back(
        dq.reshape(ROWS, 128), dkvs, raw, cosine, sine, gq, gk, normed, att, b_own, b_other, ()
    )
    terms = jnp.sum(exchange(line, DC).astype(F32), axis=0)
    lasts = sum_cores(*rows_back(graw, x_own, x_other, gain_attn, lines, tuple(came)))
    lasts = [lasts[0]] + [a.astype(BF) for a in lasts[1:]]
    packed = pack_grads(terms, gw_cols)
    cols = exchange(packed, SP)
    last = grad_middle + lasts[0]
    mixed = mixes[0] + sum(a.astype(F32) for a in came)
    came = [ring(lasts[k], "sp_0", 4 - k) for k in (1, 2, 3)]
    last += sum(a.astype(F32) for a in after(came, packed))
    rows = jnp.stack([last, mixed]).astype(BF).reshape(2, 2, 64, D).swapaxes(0, 1)
    rows = own_first(jnp.stack([rows[0], pair(rows[1], "cp_0")]), half)
    grad_tokens, mixed = rows[:, 0], rows[:, 1]

    back = [(d, s) for s, d in perm]
    gw_out = jnp.concatenate([terms[r : r + 8] for r in range(72, 104, 8)], axis=1)
    downs = lax.ppermute(jnp.concatenate([gw_out, gw_down], axis=0), DP_CP_SP, back)
    downs = after(downs, rows)
    grad_w_out, grad_w_down = downs[:8], downs[8:]
    weights = (w_query, w_key, w_value, w_gate, w_up)
    gains = (attn_gain[None], ffn_gain[None])
    *grads, grad_attn_gain, grad_ffn_gain, heads = unpack_grads(cols, weights, gains)
    grad_w_query, grad_w_key, grad_w_value, grad_w_gate, grad_w_up = grads
    return (
        mixed,
        grad_tokens,
        grad_attn_gain[0],
        grad_ffn_gain[0],
        heads,
        grad_w_query,
        grad_w_key,
        grad_w_value,
        grad_w_out,
        grad_w_gate,
        grad_w_up,
        grad_w_down,
    )


def solution(mesh):
    torus = Mesh(
        mesh.devices.reshape(mesh.shape["dp"], 2, 4, 4, 2), ("dp", "cp_0", "cp_1", "sp_0", "sp_1")
    )
    rows, split = P("dp", CP_SP, None), P(DP_CP_SP, None)
    in_specs = (rows, rows, P(), P(DP_CP_SP), P(DP_CP_SP), P()) + (split,) * 7
    out_specs = (rows, rows, P(DP_CP_SP), P(DP_CP_SP), P()) + (split,) * 7
    return jax.shard_map(
        on_device, mesh=torus, in_specs=in_specs, out_specs=out_specs, check_vma=False
    )
```
